32 devices in a mesh: groups: 2 (over x), node: 16 (over z, y, core).
Axes of the slice: x: 2, y: 2, z: 4, core: 2. Of those that a mesh axis runs over, the one named last changes fastest.
Arguments:
- tokens: bfloat16 [4096, 2048], P(('groups', 'node')), parts along dimension 0, may hold values from -6 to 6
- expert_ids: int32 [4096, 8], P(('groups', 'node')), parts along dimension 0, may hold values from 0 to 15, all different within a row; in each aligned block of 128 rows (0 to 127, 128 to 255, ...) at most 96 rows name the same one
- gate_fixed: int32 [4096, 8], P(('groups', 'node')), parts along dimension 0, may hold values from 1 to 65535
- gate_weight: bfloat16 [16, 2048, 768], P('node'), may hold values from -0.125 to 0.125
- up_weight: bfloat16 [16, 2048, 768], P('node'), may hold values from -0.125 to 0.125
- down_weight: bfloat16 [16, 768, 2048], P('node'), may hold values from -0.21875 to 0.21875
Outputs:
- mixed: bfloat16 [4096, 2048], P(('groups', 'node')), parts along dimension 0
- expert_load: float32 [32], P(('groups', 'node')), parts along dimension 0
- balance_loss: float32 [2], P('groups'), parts along dimension 0
The draws below stay inside these ranges and needn't reach their ends.
There are 2 independent parts, one for each index of `groups`. The reference program is written for one: setup_inputs(seed, part) draws one part's arguments, and reference() takes and returns one part's arrays. A program takes and returns all parts, laid end to end along the dimension named above; an argument that names none is the same for every part. Nothing has to cross between parts.
Inputs may be any that keep to these rules, and one draw needn't show every extreme that they name: `expert_ids`: each row names 8 different experts. Among the 128 rows of one device no expert is named by more than 96 rows, and in some such blocks one expert is named by exactly 96; every expert is named somewhere.
All inputs are finite; a program needn't handle non-finite values.
Results may differ from the reference program's by a relative error of at most 0.0059.
Values may be sent and summed in bfloat16 or wider, within the bound.
No kernel may reach another device: no remote copies, remote signals or barrier semaphores. Data moves between devices by JAX's collectives and lax.ppermute only.
A program may use at most 128 MiB of HBM per device.

```python
import math
import jax
import jax.numpy as jnp
import numpy as np
from jax import lax

D = 2048
FF = 768
TOP = 8
TOK_DEV = 128
EXPERTS = 16
TOKENS = 2048
CAP = 96
N_NODE = 16


def set_ends(values, key, low, largest):
    shape = values.shape
    spot = [jax.random.randint(jax.random.fold_in(key, axis), (), 0, shape[axis]) for axis in range(len(shape))]
    values = values.at[tuple(spot)].set(low)
    longest = shape.index(max(shape))
    spot[longest] = (spot[longest] + 1) % shape[longest]
    return values.at[tuple(spot)].set(largest)


def steps_of(own_key, shape, cuts, smallest, top_value):
    def one(axis_at, shards_of):
        steps = jax.random.uniform(jax.random.fold_in(jax.random.fold_in(own_key, 6), axis_at), (shards_of,), jnp.float32, smallest / len(cuts), top_value / len(cuts))
        return jnp.repeat(jnp.exp(steps), shape[axis_at] // shards_of).reshape((-1,) + (1,) * (len(shape) - axis_at - 1))

    loudness = one(*cuts[0])
    for cut in cuts[1:]:
        loudness = loudness * one(*cut)
    return loudness


def routed_block(key, own, number, rows, number_of, top, limit, skew):
    order = jax.random.permutation(key, number_of)
    heavy_load, common = load_shares(number_of, rows * top, limit, skew, True), load_shares(number_of, rows * top, limit, skew, False)
    places = jnp.arange(number_of)

    def named(lengths, turn):
        used = int((lengths > 0).sum())
        fixed = max(1, used // 4)
        shifted = fixed + (places - fixed + turn * (used - fixed)) % max(1, number_of - fixed)
        return jnp.zeros((number_of,), jnp.int32).at[order[jnp.where(places < fixed, places, shifted)]].set(jnp.asarray(lengths, jnp.int32))

    lengths = jnp.where(number % 4 == 0, named(heavy_load, number // 4), named(common, number - number // 4 - 1))
    mixed = jax.random.permutation(jax.random.fold_in(own, 3), number_of)
    source_of, taker = mixed[0:number_of // 2 * 2:2], mixed[1:number_of // 2 * 2:2]
    margin = jnp.minimum(lengths[source_of] - 1, limit - lengths[taker]) // 2
    margin = jnp.where((source_of == order[0]) | (taker == order[0]) | (lengths[taker] == 0), 0, jnp.maximum(margin, 0))
    shifted = jax.random.randint(jax.random.fold_in(own, 4), (number_of // 2,), 0, 1 << 20) % (margin + 1)
    lengths = lengths.at[source_of].add(-shifted).at[taker].add(shifted)
    items = jnp.searchsorted(jnp.cumsum(lengths), jnp.arange(rows * top), side="right").astype(jnp.int32)
    listing = items.reshape(top, rows).T
    listing = listing[jax.random.permutation(jax.random.fold_in(own, 1), rows)]
    turn = jax.random.randint(jax.random.fold_in(own, 2), (rows, 1), 0, top)
    return jnp.take_along_axis(listing, (jnp.arange(top)[None, :] + turn) % top, axis=1)


def load_shares(number_of, total, limit, skew, full):
    weights = [(1 << 20) // math.isqrt(rank ** skew) + 1 for rank in range(1, number_of + 1)]
    largest = limit if full else min(limit, max(-(-total // number_of), total * weights[0] // sum(weights)))
    least = 1 if total - largest >= number_of - 1 else 0
    holding, rest = [largest] + [least] * (number_of - 1), total - largest - least * (number_of - 1)
    while rest > 0:
        candidates = [i for i in range(1, number_of) if holding[i] < largest] or [i for i in range(1, number_of) if holding[i] < limit]
        whole, left = sum([weights[i] for i in candidates]), rest
        for i in candidates:
            more = min(limit - holding[i], max(1, left * weights[i] // whole), rest)
            holding[i] = holding[i] + more
            rest = rest - more
    return np.array(holding)


def centred(own_key, dims, spread, bound, split=(), held_as=jnp.bfloat16):
    drawn = jax.random.normal(own_key, dims, jnp.float32) * spread
    if len(split) > 0:
        drawn = steps_of(own_key, dims, split, -0.22, 0.18) * drawn
    return jnp.clip(drawn, min=-bound, max=bound).astype(held_as)


def setup_inputs(seed: int = 0, part: int = 0) -> dict:
    seeds = jax.random.split(jax.random.key(seed), 7)
    own_keys = jax.random.split(jax.random.fold_in(seeds[6], part), 7)
    tokens = centred(own_keys[0], (TOKENS, D), 1.0, 6.0, ((0, 16),))
    expert_ids_keys = jax.random.split(jax.random.fold_in(own_keys[1], 1), TOKENS // TOK_DEV)
    expert_ids_turns = jax.random.permutation(jax.random.fold_in(own_keys[1], 3), TOKENS // TOK_DEV)
    expert_ids = jax.vmap(lambda own, number: routed_block(jax.random.fold_in(own_keys[1], 2), own, number, TOK_DEV, EXPERTS, TOP, CAP, 2))(expert_ids_keys, expert_ids_turns).reshape((TOKENS, TOP))
    gate_fixed = set_ends(jax.random.randint(own_keys[2], (TOKENS, TOP), 1, 65536), jax.random.fold_in(own_keys[2], 1), 1, 65535).astype(jnp.int32)
    gate_weight = centred(seeds[3], (EXPERTS, D, FF), D ** -0.5, 0.125, ((0, 16),))
    up_weight = centred(seeds[4], (EXPERTS, D, FF), D ** -0.5, 0.125, ((0, 16),))
    down_weight = centred(seeds[5], (EXPERTS, FF, D), FF ** -0.5, 0.21875, ((0, 16),))
    return {"tokens": tokens, "expert_ids": expert_ids, "gate_fixed": gate_fixed, "gate_weight": gate_weight, "up_weight": up_weight, "down_weight": down_weight}


def expert_apply(row_block, w_gate, w_up, w_down):
    gate_value = jnp.dot(row_block, w_gate, preferred_element_type=jnp.float32)
    up_value = jnp.dot(row_block, w_up, preferred_element_type=jnp.float32)
    hidden = (jax.nn.silu(gate_value) * up_value).astype(jnp.bfloat16)
    return jnp.dot(hidden, w_down, preferred_element_type=jnp.float32).astype(jnp.bfloat16)


def reference(tokens, expert_ids, gate_fixed, gate_weight, up_weight, down_weight):
    fixed_gate = gate_fixed.astype(jnp.float32)
    weights = fixed_gate / jnp.sum(fixed_gate, axis=1, keepdims=True)
    chosen = expert_ids.reshape(-1).astype(jnp.int32)
    pair_weights = weights.reshape(-1)
    row_limit = N_NODE * CAP

    def per_expert(results, expert):
        matches = chosen == expert
        pair_index = jnp.nonzero(matches, size=row_limit, fill_value=0)[0].astype(jnp.int32)
        in_range = jnp.arange(row_limit, dtype=jnp.int32) < jnp.sum(matches.astype(jnp.int32))
        token_index = (pair_index // TOP).astype(jnp.int32)
        row_block = tokens[token_index]
        expert_out = expert_apply(row_block, gate_weight[expert], up_weight[expert], down_weight[expert])
        pair_weight = jnp.where(in_range, pair_weights[pair_index], jnp.float32(0.0))
        results = results.at[token_index].add(pair_weight[:, None] * expert_out.astype(jnp.float32))
        return results, jnp.float32(0.0)

    start = jnp.zeros((TOKENS, D), jnp.float32)
    results, unused = lax.scan(per_expert, start, jnp.arange(EXPERTS, dtype=jnp.int32))
    mixed = results.astype(jnp.bfloat16)
    counts = jax.ops.segment_sum(jnp.ones_like(pair_weights), chosen, num_segments=EXPERTS)
    gate_mass = jax.ops.segment_sum(pair_weights, chosen, num_segments=EXPERTS) / TOKENS
    expert_load = counts * EXPERTS / (TOKENS * TOP)
    balance_loss = (EXPERTS * jnp.sum(counts / (TOKENS * TOP) * gate_mass)).reshape(1)
    return mixed, expert_load, balance_loss
```

```python
import functools

import jax
import jax.numpy as jnp
from jax import lax
from jax.experimental import pallas as pl
from jax.experimental.pallas import tpu as pltpu
from jax.sharding import PartitionSpec as P

CORES = 2


def ring_order(chips):
    if chips <= 8:
        return list(range(0, chips, 2)) + list(range(1, chips, 2))[::-1]
    return list(range(chips))


def ring_shift(order, step):
    pairs = []
    for place, chip in enumerate(order):
        target = order[(place + step) % len(order)]
        pairs += [(CORES * chip + core, CORES * target + core) for core in range(CORES)]
    return pairs


def expert_kernel(hidden_steps, sizes, *refs):
    count = len(sizes)
    blocks = refs[:count]
    scale_ref, gate_ref, up_ref, down_ref = refs[count : count + 4]
    outs = refs[count + 4 : 2 * count + 4]
    rows_ref, hidden_ref, arrived = refs[2 * count + 4 :]
    step = pl.program_id(0)
    starts = [sum(sizes[:i]) for i in range(count)]
    chunk = gate_ref.shape[1]

    @pl.when(step == 0)
    def _():
        copies = [
            pltpu.make_async_copy(
                blocks[i], rows_ref.at[pl.ds(starts[i], sizes[i])], arrived.at[i]
            )
            for i in range(count)
        ]
        for copy in copies:
            copy.start()
        for copy in copies:
            copy.wait()

    for j in range(hidden_steps):

        @pl.when(step == j)
        def _():
            rows = rows_ref[...]
            gate = jnp.dot(rows, gate_ref[...], preferred_element_type=jnp.float32)
            up = jnp.dot(rows, up_ref[...], preferred_element_type=jnp.float32)
            hidden = gate / (1.0 + jnp.exp(-gate)) * up * scale_ref[...]
            hidden_ref[:, j * chunk : (j + 1) * chunk] = hidden.astype(jnp.bfloat16)

    @pl.when(step >= hidden_steps)
    def _():
        out = jnp.dot(hidden_ref[...], down_ref[...], preferred_element_type=jnp.float32)
        for i in range(count):
            outs[i][...] = out[starts[i] : starts[i] + sizes[i]].astype(jnp.bfloat16)


def apply_expert(blocks, scale, gate_weight, up_weight, down_weight):
    width, hidden_width = gate_weight.shape
    sizes = tuple(block.shape[0] for block in blocks)
    total = sum(sizes)
    count = len(blocks)
    chunk = 256
    hidden_steps = hidden_width // chunk
    out_chunk = 512
    out_steps = width // out_chunk
    first = lambda i: jnp.minimum(i, hidden_steps - 1)
    second = lambda i: jnp.maximum(i - hidden_steps, 0)
    return pl.pallas_call(
        functools.partial(expert_kernel, hidden_steps, sizes),
        grid=(hidden_steps + out_steps,),
        out_shape=[jax.ShapeDtypeStruct((size, width), jnp.bfloat16) for size in sizes],
        in_specs=[pl.BlockSpec(memory_space=pl.ANY)] * count
        + [
            pl.BlockSpec((total, 1), lambda i: (0, 0)),
            pl.BlockSpec((width, chunk), lambda i: (0, first(i))),
            pl.BlockSpec((width, chunk), lambda i: (0, first(i))),
            pl.BlockSpec((hidden_width, out_chunk), lambda i: (0, second(i))),
        ],
        out_specs=[pl.BlockSpec((size, out_chunk), lambda i: (0, second(i))) for size in sizes],
        scratch_shapes=[
            pltpu.VMEM((total, width), jnp.bfloat16),
            pltpu.VMEM((total, hidden_width), jnp.bfloat16),
            pltpu.SemaphoreType.DMA((count,)),
        ],
        compiler_params=pltpu.CompilerParams(
            vmem_limit_bytes=40 * 1024 * 1024, dimension_semantics=("arbitrary",)
        ),
        cost_estimate=pl.CostEstimate(
            flops=6 * total * width * hidden_width,
            bytes_accessed=6 * width * hidden_width + 4 * total * width,
            transcendentals=total * hidden_width,
        ),
    )(*blocks, scale, gate_weight, up_weight, down_weight)


def body(tokens, expert_ids, gate_fixed, gate_weight, up_weight, down_weight):
    tok_rows, model_width = tokens.shape
    per_token = expert_ids.shape[1]
    node_count = lax.axis_size("node")
    expert_count = node_count
    token_total = tok_rows * node_count
    chips = node_count // CORES
    far = chips // 2
    half = tok_rows // 2
    order = ring_order(chips)
    to_right, to_left = ring_shift(order, 1), ring_shift(order, -1)
    to_sibling = [(node, node ^ 1) for node in range(node_count)]
    right = lambda a: lax.ppermute(a, "node", to_right)
    left = lambda a: lax.ppermute(a, "node", to_left)
    sibling = lambda a: lax.ppermute(a, "node", to_sibling)
    node = lax.axis_index("node")
    core = node % CORES

    fixed_gate = gate_fixed.astype(jnp.float32)
    weights = fixed_gate / jnp.sum(fixed_gate, axis=1, keepdims=True)
    experts = jnp.arange(expert_count, dtype=jnp.int32)
    dense = jnp.sum(
        jnp.where(expert_ids[None] == experts[:, None, None], weights[None], 0.0), axis=2
    )
    dense_all = lax.all_gather(dense, "node")

    counts = jnp.sum((dense_all > 0).astype(jnp.float32), axis=(0, 2))
    mass = jnp.sum(dense_all, axis=(0, 2)) / token_total
    own_count = lax.dynamic_slice(counts, (node,), (1,))
    expert_load = own_count * expert_count / (token_total * per_token)
    balance_loss = (expert_count * jnp.sum(counts / (token_total * per_token) * mass)).reshape(1)

    place_of = [order.index(chip) for chip in range(chips)]
    place = jnp.asarray(place_of, jnp.int32)[node // CORES]
    offsets = [0]
    for k in range(1, far):
        offsets += [-k, k]
    offsets.append(far)
    block_chips = jnp.asarray(order, jnp.int32)[
        (place + jnp.asarray(offsets, jnp.int32)) % chips
    ]
    sources = (CORES * block_chips[:, None] + jnp.stack([core, 1 - core])[None]).reshape(-1)
    own_expert = lax.dynamic_index_in_dim(dense_all, node, 1, keepdims=False)
    scale = own_expert[sources].reshape(-1, 1)

    gate_weight, up_weight, down_weight = gate_weight[0], up_weight[0], down_weight[0]

    def run(blocks, first_row):
        total = sum(block.shape[0] for block in blocks)
        return apply_expert(
            blocks, scale[first_row : first_row + total], gate_weight, up_weight, down_weight
        )

    from_left, from_right = tokens, tokens
    mine, theirs = run([tokens, sibling(tokens)], 0)
    outs = [(mine, sibling(theirs))]
    row = 2 * tok_rows
    for k in range(1, far):
        from_left, from_right = right(from_left), left(from_right)
        res = run([from_left, sibling(from_left), from_right, sibling(from_right)], row)
        row += 4 * tok_rows
        outs.append((res[0], sibling(res[1]), res[2], sibling(res[3])))
    far_low, far_high = right(from_left[:half]), left(from_right[half:])
    res = run([far_low, far_high, sibling(far_low), sibling(far_high)], row)

    def add(*terms):
        return sum(term.astype(jnp.float32) for term in terms)

    low = left(add(res[0], sibling(res[2])).astype(jnp.bfloat16))
    high = right(add(res[1], sibling(res[3])).astype(jnp.bfloat16))
    for k in range(far - 1, 0, -1):
        left_own, left_sib, right_own, right_sib = outs[k]
        to_left_sum, to_right_sum = add(left_own, left_sib), add(right_own, right_sib)
        if k == far - 1:
            to_left_sum = to_left_sum + jnp.pad(low.astype(jnp.float32), ((0, half), (0, 0)))
            to_right_sum = to_right_sum + jnp.pad(high.astype(jnp.float32), ((half, 0), (0, 0)))
        else:
            to_left_sum = to_left_sum + low.astype(jnp.float32)
            to_right_sum = to_right_sum + high.astype(jnp.float32)
        low = left(to_left_sum.astype(jnp.bfloat16))
        high = right(to_right_sum.astype(jnp.bfloat16))
    mixed = add(*outs[0], low, high).astype(jnp.bfloat16)
    return (mixed, expert_load, balance_loss)


def solution(mesh):
    return jax.shard_map(
        body,
        mesh=mesh,
        in_specs=(
            P(("groups", "node"), None),
            P(("groups", "node"), None),
            P(("groups", "node"), None),
            P("node", None, None),
            P("node", None, None),
            P("node", None, None),
        ),
        out_specs=(P(("groups", "node"), None), P(("groups", "node")), P("groups")),
        check_vma=False,
    )
```

```python
import functools

import jax
import jax.numpy as jnp
from jax import lax
from jax.experimental import pallas as pl
from jax.experimental.pallas import tpu as pltpu
from jax.sharding import PartitionSpec as P

CORES = 2
VMEM_LIMIT = 32 * 1024 * 1024


def ring_order(chips):
    if chips <= 8:
        return list(range(0, chips, 2)) + list(range(1, chips, 2))[::-1]
    return list(range(chips))


def ring_shift(order, step):
    pairs = []
    for place, chip in enumerate(order):
        target = order[(place + step) % len(order)]
        pairs += [(CORES * chip + core, CORES * target + core) for core in range(CORES)]
    return pairs


def expert_kernel(sizes, *refs):
    count = len(sizes)
    blocks = refs[:count]
    scale_ref, gate_ref, up_ref, down_ref = refs[count : count + 4]
    outs = refs[count + 4 : 2 * count + 4]
    rows_ref, hidden_ref = refs[2 * count + 4 :]
    starts = [sum(sizes[:i]) for i in range(count)]
    width, hidden_width = gate_ref.shape
    chunk = 256

    for i in range(count):
        rows_ref[starts[i] : starts[i] + sizes[i], :] = blocks[i][...]

    @pl.loop(0, hidden_width // chunk)
    def _(j):
        at = pl.ds(pl.multiple_of(j * chunk, chunk), chunk)
        rows = rows_ref[...]
        gate = jnp.dot(rows, gate_ref[:, at], preferred_element_type=jnp.float32)
        up = jnp.dot(rows, up_ref[:, at], preferred_element_type=jnp.float32)
        hidden_ref[:, at] = (gate / (1.0 + jnp.exp(-gate)) * up).astype(jnp.bfloat16)

    @pl.loop(0, width // chunk)
    def _(j):
        at = pl.ds(pl.multiple_of(j * chunk, chunk), chunk)
        out = jnp.dot(hidden_ref[...], down_ref[:, at], preferred_element_type=jnp.float32)
        out = out.astype(jnp.bfloat16).astype(jnp.float32) * scale_ref[...]
        for i in range(count):
            outs[i][:, at] = out[starts[i] : starts[i] + sizes[i]].astype(jnp.bfloat16)


def apply_expert(blocks, scale, gate_weight, up_weight, down_weight):
    width, hidden_width = gate_weight.shape
    sizes = tuple(block.shape[0] for block in blocks)
    total = sum(sizes)
    count = len(blocks)
    in_vmem = pl.BlockSpec(memory_space=pltpu.VMEM)
    return pl.pallas_call(
        functools.partial(expert_kernel, sizes),
        out_shape=[jax.ShapeDtypeStruct((size, width), jnp.bfloat16) for size in sizes],
        in_specs=[in_vmem] * (count + 4),
        out_specs=[in_vmem] * count,
        scratch_shapes=[
            pltpu.VMEM((total, width), jnp.bfloat16),
            pltpu.VMEM((total, hidden_width), jnp.bfloat16),
        ],
        compiler_params=pltpu.CompilerParams(vmem_limit_bytes=VMEM_LIMIT),
        cost_estimate=pl.CostEstimate(
            flops=6 * total * width * hidden_width,
            bytes_accessed=4 * total * width,
            transcendentals=total * hidden_width,
        ),
    )(*blocks, scale, gate_weight, up_weight, down_weight)


def body(tokens, expert_ids, gate_fixed, gate_weight, up_weight, down_weight):
    tok_rows, model_width = tokens.shape
    per_token = expert_ids.shape[1]
    node_count = lax.axis_size("node")
    expert_count = node_count
    token_total = tok_rows * node_count
    chips = node_count // CORES
    far = chips // 2
    half = tok_rows // 2
    order = ring_order(chips)
    to_right, to_left = ring_shift(order, 1), ring_shift(order, -1)
    to_sibling = [(node, node ^ 1) for node in range(node_count)]
    right = lambda a: lax.ppermute(a, "node", to_right)
    left = lambda a: lax.ppermute(a, "node", to_left)
    sibling = lambda a: lax.ppermute(a, "node", to_sibling)
    node = lax.axis_index("node")

    fixed_gate = gate_fixed.astype(jnp.float32)
    weights = fixed_gate / jnp.sum(fixed_gate, axis=1, keepdims=True)
    experts = jnp.arange(expert_count, dtype=jnp.int32)
    dense = jnp.sum(
        jnp.where(expert_ids[None] == experts[:, None, None], weights[None], 0.0), axis=2
    )
    pair = jnp.stack([dense, sibling(dense)])
    near = [(pair,)]
    for k in range(1, far):
        near.append(
            tuple(lax.ppermute(pair, "node", ring_shift(order, step)) for step in (k, -k))
        )
    near.append((lax.ppermute(pair, "node", ring_shift(order, far)),))
    own = [
        jnp.stack([lax.dynamic_index_in_dim(p, node, 1, keepdims=False) for p in pairs])
        for pairs in near
    ]

    every = jnp.stack([p for pairs in near for p in pairs])
    counts = jnp.sum((every > 0).astype(jnp.float32), axis=(0, 1, 3))
    mass = jnp.sum(every, axis=(0, 1, 3)) / token_total
    own_count = lax.dynamic_slice(counts, (node,), (1,))
    expert_load = own_count * expert_count / (token_total * per_token)
    balance_loss = (expert_count * jnp.sum(counts / (token_total * per_token) * mass)).reshape(1)

    gate_weight, up_weight, down_weight = gate_weight[0], up_weight[0], down_weight[0]

    def run(blocks, k):
        return apply_expert(
            blocks, own[k].reshape(-1, 1), gate_weight, up_weight, down_weight
        )

    from_left, from_right = tokens, tokens
    mine, theirs = run([tokens, sibling(tokens)], 0)
    outs = [(mine, sibling(theirs))]
    for k in range(1, far):
        from_left, from_right = right(from_left), left(from_right)
        res = run([from_left, sibling(from_left), from_right, sibling(from_right)], k)
        outs.append((res[0], sibling(res[1]), res[2], sibling(res[3])))
    far_low, far_high = right(from_left[:half]), left(from_right[half:])
    res = run([far_low, far_high, sibling(far_low), sibling(far_high)], far)

    def add(*terms):
        return sum(term.astype(jnp.float32) for term in terms)

    low = left(add(res[0], sibling(res[2])).astype(jnp.bfloat16))
    high = right(add(res[1], sibling(res[3])).astype(jnp.bfloat16))
    for k in range(far - 1, 0, -1):
        left_own, left_sib, right_own, right_sib = outs[k]
        to_left_sum, to_right_sum = add(left_own, left_sib), add(right_own, right_sib)
        if k == far - 1:
            to_left_sum = to_left_sum + jnp.pad(low.astype(jnp.float32), ((0, half), (0, 0)))
            to_right_sum = to_right_sum + jnp.pad(high.astype(jnp.float32), ((half, 0), (0, 0)))
        else:
            to_left_sum = to_left_sum + low.astype(jnp.float32)
            to_right_sum = to_right_sum + high.astype(jnp.float32)
        low = left(to_left_sum.astype(jnp.bfloat16))
        high = right(to_right_sum.astype(jnp.bfloat16))
    mixed = add(*outs[0], low, high).astype(jnp.bfloat16)
    return (mixed, expert_load, balance_loss)


def solution(mesh):
    return jax.shard_map(
        body,
        mesh=mesh,
        in_specs=(
            P(("groups", "node"), None),
            P(("groups", "node"), None),
            P(("groups", "node"), None),
            P("node", None, None),
            P("node", None, None),
            P("node", None, None),
        ),
        out_specs=(P(("groups", "node"), None), P(("groups", "node")), P("groups")),
        check_vma=False,
    )
```

```python
import functools

import jax
import jax.numpy as jnp
from jax import lax
from jax.experimental import pallas as pl
from jax.experimental.pallas import tpu as pltpu
from jax.sharding import PartitionSpec as P

CORES = 2
CHUNKS = 1
LAG = 2
LANES = 128
VMEM_LIMIT = 24 * 1024 * 1024
HIDDEN_CHUNK = 256
OUT_CHUNK = 512


def ring_order(chips):
    if chips <= 8:
        return list(range(0, chips, 2)) + list(range(1, chips, 2))[::-1]
    return list(range(chips))


def ring_shift(order, step):
    pairs = []
    for place, chip in enumerate(order):
        target = order[(place + step) % len(order)]
        pairs += [(CORES * chip + core, CORES * target + core) for core in range(CORES)]
    return pairs


def pack_kernel(experts, tokens_ref, ids_ref, gates_ref, *outs):
    rows, width = tokens_ref.shape
    lanes = outs[0].shape[1] - width
    lane = lax.broadcasted_iota(jnp.int32, (rows, lanes), 1)
    ids, gates = ids_ref[...], gates_ref[...]
    scores = jnp.zeros((rows, lanes), jnp.int32)
    for k in range(ids.shape[1]):
        at, gate = ids[:, k : k + 1], gates[:, k : k + 1]
        scores = jnp.where(lane == at, gate >> 8, scores)
        scores = jnp.where(lane == at + experts, gate & 255, scores)
    scores = scores.astype(jnp.float32).astype(jnp.bfloat16)
    size = outs[0].shape[0]
    for i, out in enumerate(outs):
        out[:, :width] = tokens_ref[i * size : (i + 1) * size, :]
        out[:, width:] = scores[i * size : (i + 1) * size]


def pack(tokens, expert_ids, gate_fixed, experts, chunks):
    rows, width = tokens.shape
    lanes = -(-2 * experts // LANES) * LANES
    in_vmem = pl.BlockSpec(memory_space=pltpu.VMEM)
    return pl.pallas_call(
        functools.partial(pack_kernel, experts),
        out_shape=[jax.ShapeDtypeStruct((rows // chunks, width + lanes), jnp.bfloat16)] * chunks,
        in_specs=[in_vmem] * 3,
        out_specs=[in_vmem] * chunks,
        compiler_params=pltpu.CompilerParams(vmem_limit_bytes=VMEM_LIMIT),
        cost_estimate=pl.CostEstimate(
            flops=rows * lanes, bytes_accessed=4 * rows * width, transcendentals=0
        ),
    )(tokens, expert_ids, gate_fixed)


def expert_kernel(sizes, *refs):
    count = len(sizes)
    blocks = refs[:count]
    own_ref, join_ref, gate_ref, up_ref, down_ref = refs[count : count + 5]
    outs = refs[count + 5 : 2 * count + 5]
    stats_ref, hidden_ref = refs[2 * count + 5 :]
    starts = [sum(sizes[:i]) for i in range(count)]
    width, hidden_width = gate_ref.shape
    lanes = join_ref.shape[0]

    scores = jnp.concatenate([block[:, width:] for block in blocks], axis=0)
    joined = jnp.dot(scores, join_ref[...], preferred_element_type=jnp.float32)
    weights = joined[:, :lanes] / joined[:, lanes:]
    stats_ref[0:1, :] = jnp.sum((weights > 0).astype(jnp.float32), axis=0, keepdims=True)
    stats_ref[1:2, :] = jnp.sum(weights, axis=0, keepdims=True)
    scale = jnp.sum(weights * own_ref[...], axis=1, keepdims=True)

    rows = jnp.concatenate([block[:, :width] for block in blocks], axis=0)
    for start in range(0, hidden_width, HIDDEN_CHUNK):
        at = slice(start, start + HIDDEN_CHUNK)
        gate = jnp.dot(rows, gate_ref[:, at], preferred_element_type=jnp.float32)
        up = jnp.dot(rows, up_ref[:, at], preferred_element_type=jnp.float32)
        hidden_ref[:, at] = (gate / (1.0 + jnp.exp(-gate)) * up).astype(jnp.bfloat16)
    for start in range(0, width, OUT_CHUNK):
        at = slice(start, start + OUT_CHUNK)
        out = jnp.dot(hidden_ref[...], down_ref[:, at], preferred_element_type=jnp.float32)
        out = out.astype(jnp.bfloat16).astype(jnp.float32) * scale
        for i in range(count):
            outs[i][:, at] = out[starts[i] : starts[i] + sizes[i]].astype(jnp.bfloat16)


def apply_expert(blocks, own, join, gate_weight, up_weight, down_weight):
    width, hidden_width = gate_weight.shape
    sizes = tuple(block.shape[0] for block in blocks)
    total = sum(sizes)
    count = len(blocks)
    in_vmem = pl.BlockSpec(memory_space=pltpu.VMEM)
    return pl.pallas_call(
        functools.partial(expert_kernel, sizes),
        out_shape=[jax.ShapeDtypeStruct((size, width), jnp.bfloat16) for size in sizes]
        + [jax.ShapeDtypeStruct((2, own.shape[1]), jnp.float32)],
        in_specs=[in_vmem] * (count + 5),
        out_specs=[in_vmem] * (count + 1),
        scratch_shapes=[pltpu.VMEM((total, hidden_width), jnp.bfloat16)],
        compiler_params=pltpu.CompilerParams(vmem_limit_bytes=VMEM_LIMIT),
        cost_estimate=pl.CostEstimate(
            flops=6 * total * width * hidden_width,
            bytes_accessed=4 * total * width,
            transcendentals=total * hidden_width,
        ),
    )(*blocks, own, join, gate_weight, up_weight, down_weight)


def body(tokens, expert_ids, gate_fixed, gate_weight, up_weight, down_weight):
    tok_rows, model_width = tokens.shape
    per_token = expert_ids.shape[1]
    node_count = lax.axis_size("node")
    expert_count = node_count
    token_total = tok_rows * node_count
    chips = node_count // CORES
    far = chips // 2
    chunks = CHUNKS if chips <= 8 else 1
    half = tok_rows // chunks // 2
    order = ring_order(chips)
    to_right, to_left = ring_shift(order, 1), ring_shift(order, -1)
    to_sibling = [(node, node ^ 1) for node in range(node_count)]
    right = lambda a: lax.ppermute(a, "node", to_right)
    left = lambda a: lax.ppermute(a, "node", to_left)
    sibling = lambda a: lax.ppermute(a, "node", to_sibling)
    tie = lax.optimization_barrier
    node = lax.axis_index("node")

    packed = pack(tokens, expert_ids, gate_fixed, expert_count, chunks)
    lanes = packed[0].shape[1] - model_width
    own = (jnp.arange(lanes) == node).astype(jnp.float32)[None]
    source, target = jnp.arange(lanes)[:, None], jnp.arange(2 * lanes)[None]
    is_low = source >= expert_count
    to_expert = (target == jnp.where(is_low, source - expert_count, source)) | (target >= lanes)
    join = jnp.where(
        to_expert & (source < 2 * expert_count), jnp.where(is_low, 1.0, 256.0), 0.0
    ).astype(jnp.bfloat16)
    gate_weight, up_weight, down_weight = gate_weight[0], up_weight[0], down_weight[0]
    stats = []

    def run(blocks):
        res = apply_expert(blocks, own, join, gate_weight, up_weight, down_weight)
        stats.append(res[-1])
        return res[:-1]

    def add(*terms):
        return sum(term.astype(jnp.float32) for term in terms).astype(jnp.bfloat16)

    def give_back(outs):
        return [sibling(out) if i % 2 else out for i, out in enumerate(outs)]

    def steps(block):
        low, high = right(block), left(block)
        res = run([block, sibling(block)])
        outs = []
        for k in range(1, far):
            low, high, res = yield low, high, res
            outs.append(give_back(res))
            here = low, high
            if k < far - 1:
                low, high = right(low), left(high)
            else:
                low, high = right(low[:half]), left(high[half:])
            res = run([here[0], sibling(here[0]), here[1], sibling(here[1])])
        low, high, res = yield low, high, res
        outs.append(give_back(res))
        res = run([low, sibling(low), high, sibling(high)])
        low, low_sib, high, high_sib = give_back(res)
        low, high = add(low, low_sib), add(high, high_sib)
        for k in range(far - 1, 0, -1):
            low, high, outs = yield low, high, outs
            low, high = left(low), right(high)
            if k == far - 1:
                zeros = jnp.zeros_like(low)
                low = jnp.concatenate([low, zeros])
                high = jnp.concatenate([zeros, high])
            left_own, left_sib, right_own, right_sib = outs[k]
            low, high = add(left_own, left_sib, low), add(right_own, right_sib, high)
        low, high, outs = yield low, high, outs
        mixed.append(add(*outs[0], left(low), right(high)))

    mixed = []
    lines = [steps(block) for block in packed]
    state = [None] * chunks
    count = 2 * far + 1
    last = []
    for slot in range(count + LAG * (chunks - 1)):
        for i, line in enumerate(lines):
            step = slot - LAG * i
            if 0 <= step < count:
                try:
                    state[i] = tie(line.send(state[i]))
                except StopIteration:
                    pass

    counts, mass = sum(stats)[:, :expert_count]
    mass = mass / token_total
    own_count = lax.dynamic_slice(counts, (node,), (1,))
    expert_load = own_count * expert_count / (token_total * per_token)
    balance_loss = (expert_count * jnp.sum(counts / (token_total * per_token) * mass)).reshape(1)
    return (jnp.concatenate(mixed), expert_load, balance_loss)


def solution(mesh):
    return jax.shard_map(
        body,
        mesh=mesh,
        in_specs=(
            P(("groups", "node"), None),
            P(("groups", "node"), None),
            P(("groups", "node"), None),
            P("node", None, None),
            P("node", None, None),
            P("node", None, None),
        ),
        out_specs=(P(("groups", "node"), None), P(("groups", "node")), P("groups")),
        check_vma=False,
    )
```

```python
import functools

import jax
import jax.numpy as jnp
from jax import lax
from jax.experimental import pallas as pl
from jax.experimental.pallas import tpu as pltpu
from jax.sharding import PartitionSpec as P

CORES = 2
LANES = 128
VMEM_LIMIT = 24 * 1024 * 1024
HIDDEN_CHUNK = 256
OUT_CHUNK = 512


def ring_order(chips):
    if chips <= 8:
        return list(range(0, chips, 2)) + list(range(1, chips, 2))[::-1]
    return list(range(chips))


def ring_shift(order, step):
    pairs = []
    for place, chip in enumerate(order):
        target = order[(place + step) % len(order)]
        pairs += [(CORES * chip + core, CORES * target + core) for core in range(CORES)]
    return pairs


def pack_kernel(experts, tokens_ref, ids_ref, gates_ref, out_ref, arrived):
    rows, width = tokens_ref.shape
    lanes = out_ref.shape[1] - width
    copy = pltpu.make_async_copy(tokens_ref, out_ref.at[:, pl.ds(0, width)], arrived)
    copy.start()
    lane = lax.broadcasted_iota(jnp.int32, (lanes, rows), 0)
    scores = jnp.zeros((lanes, rows), jnp.int32)
    for k in range(ids_ref.shape[0]):
        at, gate = ids_ref[k : k + 1, :], gates_ref[k : k + 1, :]
        scores = jnp.where(lane == at, gate >> 8, scores)
        scores = jnp.where(lane == at + experts, gate & 255, scores)
    out_ref[:, width:] = scores.astype(jnp.float32).T.astype(jnp.bfloat16)
    copy.wait()


def pack(tokens, expert_ids, gate_fixed, experts):
    rows, width = tokens.shape
    lanes = -(-2 * experts // LANES) * LANES
    in_vmem = pl.BlockSpec(memory_space=pltpu.VMEM)
    return pl.pallas_call(
        functools.partial(pack_kernel, experts),
        out_shape=jax.ShapeDtypeStruct((rows, width + lanes), jnp.bfloat16),
        in_specs=[pl.BlockSpec(memory_space=pl.ANY), in_vmem, in_vmem],
        out_specs=in_vmem,
        scratch_shapes=[pltpu.SemaphoreType.DMA],
        cost_estimate=pl.CostEstimate(
            flops=rows * lanes, bytes_accessed=4 * rows * width, transcendentals=0
        ),
    )(tokens, expert_ids.T, gate_fixed.T)


def expert_kernel(sizes, *refs):
    count = len(sizes)
    blocks = refs[:count]
    own_ref, join_ref = refs[count : count + 2]
    experts = [refs[count + 2 + 3 * i : count + 5 + 3 * i] for i in range(CORES)]
    refs = refs[count + 2 + 3 * CORES :]
    outs = refs[:count]
    stats_ref, hidden_ref = refs[count:]
    starts = [sum(sizes[:i]) for i in range(count)]
    width, hidden_width = experts[0][0].shape
    lanes = join_ref.shape[0]

    scores = jnp.concatenate([block[:, width:] for block in blocks], axis=0)
    joined = jnp.dot(scores, join_ref[...], preferred_element_type=jnp.float32)
    weights = joined[:, :lanes] / joined[:, lanes:]
    stats_ref[0:1, :] = jnp.sum((weights > 0).astype(jnp.float32), axis=0, keepdims=True)
    stats_ref[1:2, :] = jnp.sum(weights, axis=0, keepdims=True)
    scales = [
        jnp.sum(weights * own_ref[i : i + 1, :], axis=1, keepdims=True) for i in range(CORES)
    ]

    rows = jnp.concatenate([block[:, :width] for block in blocks], axis=0)
    for i, (gate_ref, up_ref, _) in enumerate(experts):
        for start in range(0, hidden_width, HIDDEN_CHUNK):
            at = slice(start, start + HIDDEN_CHUNK)
            gate = jnp.dot(rows, gate_ref[:, at], preferred_element_type=jnp.float32)
            up = jnp.dot(rows, up_ref[:, at], preferred_element_type=jnp.float32)
            hidden_ref[i, :, at] = (gate / (1.0 + jnp.exp(-gate)) * up).astype(jnp.bfloat16)
    for start in range(0, width, OUT_CHUNK):
        at = slice(start, start + OUT_CHUNK)
        total = 0.0
        for i, (_, _, down_ref) in enumerate(experts):
            out = jnp.dot(hidden_ref[i], down_ref[:, at], preferred_element_type=jnp.float32)
            total = total + out.astype(jnp.bfloat16).astype(jnp.float32) * scales[i]
        for i in range(count):
            outs[i][:, at] = total[starts[i] : starts[i] + sizes[i]].astype(jnp.bfloat16)


def apply_experts(blocks, own, join, weights):
    width, hidden_width = weights[0].shape
    sizes = tuple(block.shape[0] for block in blocks)
    total = sum(sizes)
    count = len(blocks)
    in_vmem = pl.BlockSpec(memory_space=pltpu.VMEM)
    return pl.pallas_call(
        functools.partial(expert_kernel, sizes),
        out_shape=[jax.ShapeDtypeStruct((size, width), jnp.bfloat16) for size in sizes]
        + [jax.ShapeDtypeStruct((2, own.shape[1]), jnp.float32)],
        in_specs=[in_vmem] * (count + 2 + len(weights)),
        out_specs=[in_vmem] * (count + 1),
        scratch_shapes=[pltpu.VMEM((CORES, total, hidden_width), jnp.bfloat16)],
        compiler_params=pltpu.CompilerParams(vmem_limit_bytes=VMEM_LIMIT),
        cost_estimate=pl.CostEstimate(
            flops=6 * CORES * total * width * hidden_width,
            bytes_accessed=4 * total * width,
            transcendentals=CORES * total * hidden_width,
        ),
    )(*blocks, own, join, *weights)


def body(tokens, expert_ids, gate_fixed, gate_weight, up_weight, down_weight):
    tok_rows, model_width = tokens.shape
    per_token = expert_ids.shape[1]
    node_count = lax.axis_size("node")
    expert_count = node_count
    token_total = tok_rows * node_count
    chips = node_count // CORES
    far = chips // 2
    half = tok_rows // 2
    order = ring_order(chips)
    to_right, to_left = ring_shift(order, 1), ring_shift(order, -1)
    to_sibling = [(node, node ^ 1) for node in range(node_count)]
    right = lambda a: lax.ppermute(a, "node", to_right)
    left = lambda a: lax.ppermute(a, "node", to_left)
    sibling = lambda a: lax.ppermute(a, "node", to_sibling)
    tie = lax.optimization_barrier
    node = lax.axis_index("node")

    weights = [gate_weight[0], up_weight[0], down_weight[0]]
    weights += [sibling(weight) for weight in weights]
    packed = pack(tokens, expert_ids, gate_fixed, expert_count)
    lanes = packed.shape[1] - model_width
    own = (jnp.arange(lanes)[None] == jnp.stack([node, node ^ 1])[:, None]).astype(jnp.float32)
    source, target = jnp.arange(lanes)[:, None], jnp.arange(2 * lanes)[None]
    is_low = source >= expert_count
    to_expert = (target == jnp.where(is_low, source - expert_count, source)) | (target >= lanes)
    join = jnp.where(
        to_expert & (source < 2 * expert_count), jnp.where(is_low, 1.0, 256.0), 0.0
    ).astype(jnp.bfloat16)
    stats = []

    def run(blocks):
        res = apply_experts(blocks, own, join, weights)
        stats.append(res[-1])
        return res[:-1]

    def add(*terms):
        return sum(term.astype(jnp.float32) for term in terms).astype(jnp.bfloat16)

    low, high = right(packed), left(packed)
    blocks, outs, fresh = {}, {}, {}
    for step in range(2, far + 1):
        (low, high), fresh = tie(((low, high), fresh))
        outs.update(fresh)
        blocks[step - 1] = (low, high)
        if step < far:
            low, high = right(low), left(high)
        else:
            low, high = right(low[:half]), left(high[half:])
        ready = [k for k in blocks if k not in outs] if step >= min(3, far) else []
        fresh = {k: run(blocks[k]) for k in ready}
    (low, high), fresh = tie(((low, high), fresh))
    outs.update(fresh)
    low, high = run([low, high])

    low, high, packed = tie((low, high, packed))
    (own_rows,) = run([packed])
    for k in range(far - 1, 0, -1):
        low, high = left(low), right(high)
        if k == far - 1:
            zeros = jnp.zeros_like(low)
            low = jnp.concatenate([low, zeros])
            high = jnp.concatenate([zeros, high])
        low, high = tie((add(outs[k][0], low), add(outs[k][1], high)))
    mixed = add(own_rows, left(low), right(high))

    total = sum(stats)
    counts, mass = (total + sibling(total))[:, :expert_count]
    mass = mass / token_total
    own_count = lax.dynamic_slice(counts, (node,), (1,))
    expert_load = own_count * expert_count / (token_total * per_token)
    balance_loss = (expert_count * jnp.sum(counts / (token_total * per_token) * mass)).reshape(1)
    return (mixed, expert_load, balance_loss)


def solution(mesh):
    return jax.shard_map(
        body,
        mesh=mesh,
        in_specs=(
            P(("groups", "node"), None),
            P(("groups", "node"), None),
            P(("groups", "node"), None),
            P("node", None, None),
            P("node", None, None),
            P("node", None, None),
        ),
        out_specs=(P(("groups", "node"), None), P(("groups", "node")), P("groups")),
        check_vma=False,
    )
```

```python
import functools

import jax
import jax.numpy as jnp
from jax import lax
from jax.experimental import pallas as pl
from jax.experimental.pallas import tpu as pltpu
from jax.sharding import PartitionSpec as P

CORES = 2
LANES = 128
VMEM_LIMIT = 20 * 1024 * 1024
HIDDEN_CHUNK = 256
OUT_CHUNK = 512


def ring_order(chips):
    if chips <= 8:
        return list(range(0, chips, 2)) + list(range(1, chips, 2))[::-1]
    return list(range(chips))


def ring_shift(order, step):
    pairs = []
    for place, chip in enumerate(order):
        target = order[(place + step) % len(order)]
        pairs += [(CORES * chip + core, CORES * target + core) for core in range(CORES)]
    return pairs


def pack_kernel(experts, tokens_ref, ids_ref, gates_ref, out_ref, arrived):
    rows, width = tokens_ref.shape
    lanes = out_ref.shape[1] - width
    copy = pltpu.make_async_copy(tokens_ref, out_ref.at[:, pl.ds(0, width)], arrived)
    copy.start()
    lane = lax.broadcasted_iota(jnp.int32, (lanes, rows), 0)
    scores = jnp.zeros((lanes, rows), jnp.int32)
    for k in range(ids_ref.shape[0]):
        at, gate = ids_ref[k : k + 1, :], gates_ref[k : k + 1, :]
        scores = jnp.where(lane == at, gate >> 8, scores)
        scores = jnp.where(lane == at + experts, gate & 255, scores)
    out_ref[:, width:] = scores.astype(jnp.float32).T.astype(jnp.bfloat16)
    copy.wait()


def pack(tokens, expert_ids, gate_fixed, experts):
    rows, width = tokens.shape
    lanes = -(-2 * experts // LANES) * LANES
    in_vmem = pl.BlockSpec(memory_space=pltpu.VMEM)
    return pl.pallas_call(
        functools.partial(pack_kernel, experts),
        out_shape=jax.ShapeDtypeStruct((rows, width + lanes), jnp.bfloat16),
        in_specs=[pl.BlockSpec(memory_space=pl.ANY), in_vmem, in_vmem],
        out_specs=in_vmem,
        scratch_shapes=[pltpu.SemaphoreType.DMA],
        cost_estimate=pl.CostEstimate(
            flops=rows * lanes, bytes_accessed=4 * rows * width, transcendentals=0
        ),
    )(tokens, expert_ids.T, gate_fixed.T)


def expert_kernel(sizes, *refs):
    count = len(sizes)
    blocks = refs[:count]
    own_ref, join_ref = refs[count : count + 2]
    own_weights, far_weights = refs[count + 2 : count + 5], refs[count + 5 : count + 8]
    outs = refs[count + 8 : 2 * count + 8]
    stats_ref, hidden_ref, *held, arrived = refs[2 * count + 8 :]
    experts = [own_weights, held]
    starts = [sum(sizes[:i]) for i in range(count)]
    width, hidden_width = own_weights[0].shape
    lanes = join_ref.shape[0]

    copies = [
        pltpu.make_async_copy(far_weights[i], held[i], arrived.at[i]) for i in range(len(held))
    ]
    for copy in copies:
        copy.start()

    scores = jnp.concatenate([block[:, width:] for block in blocks], axis=0)
    joined = jnp.dot(scores, join_ref[...], preferred_element_type=jnp.float32)
    weights = joined[:, :lanes] / joined[:, lanes:]
    stats_ref[0:1, :] = jnp.sum((weights > 0).astype(jnp.float32), axis=0, keepdims=True)
    stats_ref[1:2, :] = jnp.sum(weights, axis=0, keepdims=True)
    scales = [
        jnp.sum(weights * own_ref[i : i + 1, :], axis=1, keepdims=True) for i in range(CORES)
    ]

    rows = jnp.concatenate([block[:, :width] for block in blocks], axis=0)
    for i, (gate_ref, up_ref, _) in enumerate(experts):
        if i:
            copies[0].wait()
            copies[1].wait()
        for start in range(0, hidden_width, HIDDEN_CHUNK):
            at = slice(start, start + HIDDEN_CHUNK)
            gate = jnp.dot(rows, gate_ref[:, at], preferred_element_type=jnp.float32)
            up = jnp.dot(rows, up_ref[:, at], preferred_element_type=jnp.float32)
            hidden_ref[i, :, at] = (gate / (1.0 + jnp.exp(-gate)) * up).astype(jnp.bfloat16)
    copies[2].wait()
    for start in range(0, width, OUT_CHUNK):
        at = slice(start, start + OUT_CHUNK)
        total = 0.0
        for i, (_, _, down_ref) in enumerate(experts):
            out = jnp.dot(hidden_ref[i], down_ref[:, at], preferred_element_type=jnp.float32)
            total = total + out.astype(jnp.bfloat16).astype(jnp.float32) * scales[i]
        for i in range(count):
            outs[i][:, at] = total[starts[i] : starts[i] + sizes[i]].astype(jnp.bfloat16)


def apply_experts(blocks, own, join, weights):
    width, hidden_width = weights[0].shape
    sizes = tuple(block.shape[0] for block in blocks)
    total = sum(sizes)
    count = len(blocks)
    in_vmem = pl.BlockSpec(memory_space=pltpu.VMEM)
    return pl.pallas_call(
        functools.partial(expert_kernel, sizes),
        out_shape=[jax.ShapeDtypeStruct((size, width), jnp.bfloat16) for size in sizes]
        + [jax.ShapeDtypeStruct((2, own.shape[1]), jnp.float32)],
        in_specs=[in_vmem] * (count + 5) + [pl.BlockSpec(memory_space=pl.ANY)] * 3,
        out_specs=[in_vmem] * (count + 1),
        scratch_shapes=[pltpu.VMEM((CORES, total, hidden_width), jnp.bfloat16)]
        + [pltpu.VMEM(weight.shape, jnp.bfloat16) for weight in weights[3:]]
        + [pltpu.SemaphoreType.DMA((3,))],
        compiler_params=pltpu.CompilerParams(vmem_limit_bytes=VMEM_LIMIT),
        cost_estimate=pl.CostEstimate(
            flops=6 * CORES * total * width * hidden_width,
            bytes_accessed=4 * total * width,
            transcendentals=CORES * total * hidden_width,
        ),
    )(*blocks, own, join, *weights)


def body(tokens, expert_ids, gate_fixed, gate_weight, up_weight, down_weight):
    tok_rows, model_width = tokens.shape
    per_token = expert_ids.shape[1]
    node_count = lax.axis_size("node")
    expert_count = node_count
    token_total = tok_rows * node_count
    chips = node_count // CORES
    far = chips // 2
    half = tok_rows // 2
    order = ring_order(chips)
    to_right, to_left = ring_shift(order, 1), ring_shift(order, -1)
    to_sibling = [(node, node ^ 1) for node in range(node_count)]
    right = lambda a: lax.ppermute(a, "node", to_right)
    left = lambda a: lax.ppermute(a, "node", to_left)
    sibling = lambda a: lax.ppermute(a, "node", to_sibling)
    tie = lax.optimization_barrier
    node = lax.axis_index("node")

    weights = [gate_weight[0], up_weight[0], down_weight[0]]
    weights += [sibling(weight) for weight in weights]
    packed = pack(tokens, expert_ids, gate_fixed, expert_count)
    lanes = packed.shape[1] - model_width
    own = (jnp.arange(lanes)[None] == jnp.stack([node, node ^ 1])[:, None]).astype(jnp.float32)
    source, target = jnp.arange(lanes)[:, None], jnp.arange(2 * lanes)[None]
    is_low = source >= expert_count
    to_expert = (target == jnp.where(is_low, source - expert_count, source)) | (target >= lanes)
    join = jnp.where(
        to_expert & (source < 2 * expert_count), jnp.where(is_low, 1.0, 256.0), 0.0
    ).astype(jnp.bfloat16)
    stats = []

    def run(blocks):
        res = apply_experts(blocks, own, join, weights)
        stats.append(res[-1])
        return res[:-1]

    def add(*terms):
        return sum(term.astype(jnp.float32) for term in terms).astype(jnp.bfloat16)

    low, high = right(packed), left(packed)
    outs = {}
    for k in range(1, far + 1):
        if k > 1:
            low, high, outs[k - 1] = tie((low, high, outs[k - 1]))
        here = low, high
        if k == far:
            break
        if k < far - 1:
            low, high = right(low), left(high)
        else:
            low, high = right(low[:half]), left(high[half:])
        outs[k] = run(here)
    low, high = run(here)

    low, high, packed = tie((low, high, packed))
    (own_rows,) = run([packed])
    for k in range(far - 1, 0, -1):
        low, high = left(low), right(high)
        if k == far - 1:
            zeros = jnp.zeros_like(low)
            low = jnp.concatenate([low, zeros])
            high = jnp.concatenate([zeros, high])
        low, high = ((add(outs[k][0], low), add(outs[k][1], high)))
    mixed = add(own_rows, left(low), right(high))

    total = sum(stats)
    counts, mass = (total + sibling(total))[:, :expert_count]
    mass = mass / token_total
    own_count = lax.dynamic_slice(counts, (node,), (1,))
    expert_load = own_count * expert_count / (token_total * per_token)
    balance_loss = (expert_count * jnp.sum(counts / (token_total * per_token) * mass)).reshape(1)
    return (mixed, expert_load, balance_loss)


def solution(mesh):
    return jax.shard_map(
        body,
        mesh=mesh,
        in_specs=(
            P(("groups", "node"), None),
            P(("groups", "node"), None),
            P(("groups", "node"), None),
            P("node", None, None),
            P("node", None, None),
            P("node", None, None),
        ),
        out_specs=(P(("groups", "node"), None), P(("groups", "node")), P("groups")),
        check_vma=False,
    )
```

```python
import functools

import jax
import jax.numpy as jnp
from jax import lax
from jax.experimental import pallas as pl
from jax.experimental.pallas import tpu as pltpu
from jax.sharding import PartitionSpec as P

CORES = 2
LANES = 128
VMEM_LIMIT = 10 * 1024 * 1024
HIDDEN_CHUNK = 256
OUT_CHUNK = 512


def ring_order(chips):
    if chips <= 8:
        return list(range(0, chips, 2)) + list(range(1, chips, 2))[::-1]
    return list(range(chips))


def ring_shift(order, step):
    pairs = []
    for place, chip in enumerate(order):
        target = order[(place + step) % len(order)]
        pairs += [(CORES * chip + core, CORES * target + core) for core in range(CORES)]
    return pairs


def pack_kernel(experts, tokens_ref, ids_hbm, gates_hbm, out_ref, ids_ref, gates_ref, arrived):
    rows, width = tokens_ref.shape
    lanes = out_ref.shape[1] - width
    copies = [
        pltpu.make_async_copy(ids_hbm, ids_ref, arrived.at[0]),
        pltpu.make_async_copy(gates_hbm, gates_ref, arrived.at[1]),
        pltpu.make_async_copy(tokens_ref, out_ref.at[:, pl.ds(0, width)], arrived.at[2]),
    ]
    for copy in copies:
        copy.start()
    copies[0].wait()
    copies[1].wait()
    lane = lax.broadcasted_iota(jnp.int32, (lanes, rows), 0)
    scores = jnp.zeros((lanes, rows), jnp.int32)
    for k in range(ids_ref.shape[0]):
        at, gate = ids_ref[k : k + 1, :], gates_ref[k : k + 1, :]
        scores = jnp.where(lane == at, gate >> 8, scores)
        scores = jnp.where(lane == at + experts, gate & 255, scores)
    out_ref[:, width:] = scores.astype(jnp.float32).T.astype(jnp.bfloat16)
    copies[2].wait()


def pack(tokens, expert_ids, gate_fixed, experts):
    rows, width = tokens.shape
    lanes = -(-2 * experts // LANES) * LANES
    per_token = expert_ids.shape[1]
    return pl.pallas_call(
        functools.partial(pack_kernel, experts),
        out_shape=jax.ShapeDtypeStruct((rows, width + lanes), jnp.bfloat16),
        in_specs=[pl.BlockSpec(memory_space=pl.ANY)] * 3,
        out_specs=pl.BlockSpec(memory_space=pltpu.VMEM),
        scratch_shapes=[
            pltpu.VMEM((per_token, rows), jnp.int32),
            pltpu.VMEM((per_token, rows), jnp.int32),
            pltpu.SemaphoreType.DMA((3,)),
        ],
        cost_estimate=pl.CostEstimate(
            flops=rows * lanes, bytes_accessed=4 * rows * width, transcendentals=0
        ),
    )(tokens, expert_ids.T, gate_fixed.T)


def hold_kernel(*refs):
    count = len(refs) // 2
    arrived = refs[-1]
    copies = [
        pltpu.make_async_copy(refs[i], refs[count + i], arrived.at[i]) for i in range(count)
    ]
    for copy in copies:
        copy.start()
    for copy in copies:
        copy.wait()


def hold(arrays):
    return pl.pallas_call(
        hold_kernel,
        out_shape=[pltpu.VMEM(array.shape, array.dtype) for array in arrays],
        in_specs=[pl.BlockSpec(memory_space=pl.ANY)] * len(arrays),
        out_specs=[pl.BlockSpec(memory_space=pltpu.VMEM)] * len(arrays),
        scratch_shapes=[pltpu.SemaphoreType.DMA((len(arrays),))],
        compiler_params=pltpu.CompilerParams(vmem_limit_bytes=VMEM_LIMIT),
    )(*arrays)


def expert_kernel(sizes, *refs):
    count = len(sizes)
    blocks = refs[:count]
    own_ref, join_ref = refs[count : count + 2]
    experts = [refs[count + 2 + 3 * i : count + 5 + 3 * i] for i in range(CORES)]
    refs = refs[count + 2 + 3 * CORES :]
    outs = refs[:count]
    stats_ref, hidden_ref = refs[count:]
    starts = [sum(sizes[:i]) for i in range(count)]
    width, hidden_width = experts[0][0].shape
    lanes = join_ref.shape[0]

    scores = jnp.concatenate([block[:, width:] for block in blocks], axis=0)
    joined = jnp.dot(scores, join_ref[...], preferred_element_type=jnp.float32)
    weights = joined[:, :lanes] / joined[:, lanes:]
    stats_ref[0:1, :] = jnp.sum((weights > 0).astype(jnp.float32), axis=0, keepdims=True)
    stats_ref[1:2, :] = jnp.sum(weights, axis=0, keepdims=True)
    scales = [
        jnp.sum(weights * own_ref[i : i + 1, :], axis=1, keepdims=True) for i in range(CORES)
    ]

    rows = jnp.concatenate([block[:, :width] for block in blocks], axis=0)
    for i, (gate_ref, up_ref, _) in enumerate(experts):
        for start in range(0, hidden_width, HIDDEN_CHUNK):
            at = slice(start, start + HIDDEN_CHUNK)
            gate = jnp.dot(rows, gate_ref[:, at], preferred_element_type=jnp.float32)
            up = jnp.dot(rows, up_ref[:, at], preferred_element_type=jnp.float32)
            hidden_ref[i, :, at] = (gate / (1.0 + jnp.exp(-gate)) * up).astype(jnp.bfloat16)
    for start in range(0, width, OUT_CHUNK):
        at = slice(start, start + OUT_CHUNK)
        total = 0.0
        for i, (_, _, down_ref) in enumerate(experts):
            out = jnp.dot(hidden_ref[i], down_ref[:, at], preferred_element_type=jnp.float32)
            total = total + out.astype(jnp.bfloat16).astype(jnp.float32) * scales[i]
        for i in range(count):
            outs[i][:, at] = total[starts[i] : starts[i] + sizes[i]].astype(jnp.bfloat16)


def apply_experts(blocks, own, join, weights):
    width, hidden_width = weights[0].shape
    sizes = tuple(block.shape[0] for block in blocks)
    total = sum(sizes)
    count = len(blocks)
    in_vmem = pl.BlockSpec(memory_space=pltpu.VMEM)
    return pl.pallas_call(
        functools.partial(expert_kernel, sizes),
        out_shape=[jax.ShapeDtypeStruct((size, width), jnp.bfloat16) for size in sizes]
        + [jax.ShapeDtypeStruct((2, own.shape[1]), jnp.float32)],
        in_specs=[in_vmem] * (count + 2 + len(weights)),
        out_specs=[in_vmem] * (count + 1),
        scratch_shapes=[pltpu.VMEM((CORES, total, hidden_width), jnp.bfloat16)],
        compiler_params=pltpu.CompilerParams(vmem_limit_bytes=VMEM_LIMIT),
        cost_estimate=pl.CostEstimate(
            flops=6 * CORES * total * width * hidden_width,
            bytes_accessed=4 * total * width,
            transcendentals=CORES * total * hidden_width,
        ),
    )(*blocks, own, join, *weights)


def body(tokens, expert_ids, gate_fixed, gate_weight, up_weight, down_weight):
    tok_rows, model_width = tokens.shape
    per_token = expert_ids.shape[1]
    node_count = lax.axis_size("node")
    expert_count = node_count
    token_total = tok_rows * node_count
    chips = node_count // CORES
    far = chips // 2
    half = tok_rows // 2
    order = ring_order(chips)
    to_right, to_left = ring_shift(order, 1), ring_shift(order, -1)
    to_sibling = [(node, node ^ 1) for node in range(node_count)]
    right = lambda a: lax.ppermute(a, "node", to_right)
    left = lambda a: lax.ppermute(a, "node", to_left)
    sibling = lambda a: lax.ppermute(a, "node", to_sibling)
    tie = lax.optimization_barrier
    node = lax.axis_index("node")

    weights = [gate_weight[0], up_weight[0], down_weight[0]]
    others = [sibling(weight) for weight in weights]
    weights = hold([pltpu.with_memory_space_constraint(w, pltpu.HBM) for w in weights + others])
    packed = pack(tokens, expert_ids, gate_fixed, expert_count)
    lanes = packed.shape[1] - model_width
    own = (jnp.arange(lanes)[None] == jnp.stack([node, node ^ 1])[:, None]).astype(jnp.float32)
    source, target = jnp.arange(lanes)[:, None], jnp.arange(2 * lanes)[None]
    is_low = source >= expert_count
    to_expert = (target == jnp.where(is_low, source - expert_count, source)) | (target >= lanes)
    join = jnp.where(
        to_expert & (source < 2 * expert_count), jnp.where(is_low, 1.0, 256.0), 0.0
    ).astype(jnp.bfloat16)
    stats = []

    def run(blocks):
        res = apply_experts(blocks, own, join, weights)
        stats.append(res[-1])
        return res[:-1]

    def add(*terms):
        return sum(term.astype(jnp.float32) for term in terms).astype(jnp.bfloat16)

    low, high = right(packed), left(packed)
    outs = {}
    for k in range(1, far + 1):
        if k > 1:
            low, high, outs[k - 1] = tie((low, high, outs[k - 1]))
        here = low, high
        if k == far:
            break
        if k < far - 1:
            low, high = right(low), left(high)
        else:
            low, high = right(low[:half]), left(high[half:])
        outs[k] = run(here)
    low, high = run(here)

    low, high, packed = tie((low, high, packed))
    (own_rows,) = run([packed])
    for k in range(far - 1, 0, -1):
        low, high = left(low), right(high)
        if k == far - 1:
            zeros = jnp.zeros_like(low)
            low = jnp.concatenate([low, zeros])
            high = jnp.concatenate([zeros, high])
        low, high = ((add(outs[k][0], low), add(outs[k][1], high)))
    mixed = add(own_rows, left(low), right(high))

    total = sum(stats)
    counts, mass = (total + sibling(total))[:, :expert_count]
    mass = mass / token_total
    own_count = lax.dynamic_slice(counts, (node,), (1,))
    expert_load = own_count * expert_count / (token_total * per_token)
    balance_loss = (expert_count * jnp.sum(counts / (token_total * per_token) * mass)).reshape(1)
    return (mixed, expert_load, balance_loss)


def solution(mesh):
    return jax.shard_map(
        body,
        mesh=mesh,
        in_specs=(
            P(("groups", "node"), None),
            P(("groups", "node"), None),
            P(("groups", "node"), None),
            P("node", None, None),
            P("node", None, None),
            P("node", None, None),
        ),
        out_specs=(P(("groups", "node"), None), P(("groups", "node")), P("groups")),
        check_vma=False,
    )
```

```python
import functools

import jax
import jax.numpy as jnp
from jax import lax
from jax.experimental import pallas as pl
from jax.experimental.pallas import tpu as pltpu
from jax.sharding import PartitionSpec as P

CORES = 2
LANES = 128
VMEM_LIMIT = 10 * 1024 * 1024
HIDDEN_CHUNK = 256
OUT_CHUNK = 512


def ring_order(chips):
    if chips <= 8:
        return list(range(0, chips, 2)) + list(range(1, chips, 2))[::-1]
    return list(range(chips))


def ring_shift(order, step):
    pairs = []
    for place, chip in enumerate(order):
        target = order[(place + step) % len(order)]
        pairs += [(CORES * chip + core, CORES * target + core) for core in range(CORES)]
    return pairs


def pack_kernel(experts, tokens_ref, ids_hbm, gates_hbm, out_ref, ids_ref, gates_ref, arrived):
    rows, width = tokens_ref.shape
    lanes = out_ref.shape[1] - width
    copies = [
        pltpu.make_async_copy(ids_hbm, ids_ref, arrived.at[0]),
        pltpu.make_async_copy(gates_hbm, gates_ref, arrived.at[1]),
        pltpu.make_async_copy(tokens_ref, out_ref.at[:, pl.ds(0, width)], arrived.at[2]),
    ]
    for copy in copies:
        copy.start()
    copies[0].wait()
    copies[1].wait()
    lane = lax.broadcasted_iota(jnp.int32, (lanes, rows), 0)
    scores = jnp.zeros((lanes, rows), jnp.int32)
    for k in range(ids_ref.shape[0]):
        at, gate = ids_ref[k : k + 1, :], gates_ref[k : k + 1, :]
        scores = jnp.where(lane == at, gate >> 8, scores)
        scores = jnp.where(lane == at + experts, gate & 255, scores)
    out_ref[:, width:] = scores.astype(jnp.float32).T.astype(jnp.bfloat16)
    copies[2].wait()


def pack(tokens, expert_ids, gate_fixed, experts):
    rows, width = tokens.shape
    lanes = -(-2 * experts // LANES) * LANES
    per_token = expert_ids.shape[1]
    return pl.pallas_call(
        functools.partial(pack_kernel, experts),
        out_shape=jax.ShapeDtypeStruct((rows, width + lanes), jnp.bfloat16),
        in_specs=[pl.BlockSpec(memory_space=pl.ANY)] * 3,
        out_specs=pl.BlockSpec(memory_space=pltpu.VMEM),
        scratch_shapes=[
            pltpu.VMEM((per_token, rows), jnp.int32),
            pltpu.VMEM((per_token, rows), jnp.int32),
            pltpu.SemaphoreType.DMA((3,)),
        ],
        cost_estimate=pl.CostEstimate(
            flops=rows * lanes, bytes_accessed=4 * rows * width, transcendentals=0
        ),
    )(tokens, expert_ids.T, gate_fixed.T)


def join_kernel(*refs):
    out_ref = refs[-1]
    half = out_ref.shape[0] // 2
    for i in range(2):
        total = sum(ref[...].astype(jnp.float32) for ref in refs[3 * i : 3 * i + 3])
        out_ref[i * half : (i + 1) * half, :] = total.astype(jnp.bfloat16)


def join_halves(first, second):
    rows, width = first[0].shape
    in_vmem = pl.BlockSpec(memory_space=pltpu.VMEM)
    return pl.pallas_call(
        join_kernel,
        out_shape=jax.ShapeDtypeStruct((2 * rows, width), jnp.bfloat16),
        in_specs=[in_vmem] * 6,
        out_specs=in_vmem,
        compiler_params=pltpu.CompilerParams(vmem_limit_bytes=VMEM_LIMIT // 2),
    )(*first, *second)


def hold_kernel(*refs):
    count = len(refs) // 2
    arrived = refs[-1]
    copies = [
        pltpu.make_async_copy(refs[i], refs[count + i], arrived.at[i]) for i in range(count)
    ]
    for copy in copies:
        copy.start()
    for copy in copies:
        copy.wait()


def hold(arrays):
    return pl.pallas_call(
        hold_kernel,
        out_shape=[pltpu.VMEM(array.shape, array.dtype) for array in arrays],
        in_specs=[pl.BlockSpec(memory_space=pl.ANY)] * len(arrays),
        out_specs=[pl.BlockSpec(memory_space=pltpu.VMEM)] * len(arrays),
        scratch_shapes=[pltpu.SemaphoreType.DMA((len(arrays),))],
        compiler_params=pltpu.CompilerParams(vmem_limit_bytes=VMEM_LIMIT),
    )(*arrays)


def expert_kernel(sizes, piece, *refs):
    count = len(sizes)
    blocks = refs[:count]
    own_ref, join_ref = refs[count : count + 2]
    experts = [refs[count + 2 + 3 * i : count + 5 + 3 * i] for i in range(CORES)]
    refs = refs[count + 2 + 3 * CORES :]
    *outs, stats_ref, hidden_ref = refs
    width, hidden_width = experts[0][0].shape
    lanes = join_ref.shape[0]

    scores = jnp.concatenate([block[:, width:] for block in blocks], axis=0)
    joined = jnp.dot(scores, join_ref[...], preferred_element_type=jnp.float32)
    weights = joined[:, :lanes] / joined[:, lanes:]
    stats_ref[0:1, :] = jnp.sum((weights > 0).astype(jnp.float32), axis=0, keepdims=True)
    stats_ref[1:2, :] = jnp.sum(weights, axis=0, keepdims=True)
    scales = [
        jnp.sum(weights * own_ref[i : i + 1, :], axis=1, keepdims=True) for i in range(CORES)
    ]

    rows = jnp.concatenate([block[:, :width] for block in blocks], axis=0)
    for i, (gate_ref, up_ref, _) in enumerate(experts):
        for start in range(0, hidden_width, HIDDEN_CHUNK):
            at = slice(start, start + HIDDEN_CHUNK)
            gate = jnp.dot(rows, gate_ref[:, at], preferred_element_type=jnp.float32)
            up = jnp.dot(rows, up_ref[:, at], preferred_element_type=jnp.float32)
            hidden_ref[i, :, at] = (gate / (1.0 + jnp.exp(-gate)) * up).astype(jnp.bfloat16)
    for start in range(0, width, OUT_CHUNK):
        at = slice(start, start + OUT_CHUNK)
        total = 0.0
        for i, (_, _, down_ref) in enumerate(experts):
            out = jnp.dot(hidden_ref[i], down_ref[:, at], preferred_element_type=jnp.float32)
            total = total + out.astype(jnp.bfloat16).astype(jnp.float32) * scales[i]
        for i, out_ref in enumerate(outs):
            out_ref[:, at] = total[i * piece : (i + 1) * piece].astype(jnp.bfloat16)


def apply_experts(blocks, piece, own, join, weights):
    width, hidden_width = weights[0].shape
    sizes = tuple(block.shape[0] for block in blocks)
    total = sum(sizes)
    count = len(blocks)
    in_vmem = pl.BlockSpec(memory_space=pltpu.VMEM)
    return pl.pallas_call(
        functools.partial(expert_kernel, sizes, piece),
        out_shape=[jax.ShapeDtypeStruct((piece, width), jnp.bfloat16)] * (total // piece)
        + [jax.ShapeDtypeStruct((2, own.shape[1]), jnp.float32)],
        in_specs=[in_vmem] * (count + 2 + len(weights)),
        out_specs=[in_vmem] * (total // piece + 1),
        scratch_shapes=[pltpu.VMEM((CORES, total, hidden_width), jnp.bfloat16)],
        compiler_params=pltpu.CompilerParams(vmem_limit_bytes=VMEM_LIMIT),
        cost_estimate=pl.CostEstimate(
            flops=6 * CORES * total * width * hidden_width,
            bytes_accessed=4 * total * width,
            transcendentals=CORES * total * hidden_width,
        ),
    )(*blocks, own, join, *weights)


def body(tokens, expert_ids, gate_fixed, gate_weight, up_weight, down_weight):
    tok_rows, model_width = tokens.shape
    per_token = expert_ids.shape[1]
    node_count = lax.axis_size("node")
    expert_count = node_count
    token_total = tok_rows * node_count
    chips = node_count // CORES
    far = chips // 2
    half = tok_rows // 2
    order = ring_order(chips)
    to_right, to_left = ring_shift(order, 1), ring_shift(order, -1)
    to_sibling = [(node, node ^ 1) for node in range(node_count)]
    right = lambda a: lax.ppermute(a, "node", to_right)
    left = lambda a: lax.ppermute(a, "node", to_left)
    sibling = lambda a: lax.ppermute(a, "node", to_sibling)
    tie = lax.optimization_barrier
    node = lax.axis_index("node")

    weights = [gate_weight[0], up_weight[0], down_weight[0]]
    others = [sibling(weight) for weight in weights]
    weights = hold([pltpu.with_memory_space_constraint(w, pltpu.HBM) for w in weights + others])
    packed = pack(tokens, expert_ids, gate_fixed, expert_count)
    lanes = packed.shape[1] - model_width
    own = (jnp.arange(lanes)[None] == jnp.stack([node, node ^ 1])[:, None]).astype(jnp.float32)
    source, target = jnp.arange(lanes)[:, None], jnp.arange(2 * lanes)[None]
    is_low = source >= expert_count
    to_expert = (target == jnp.where(is_low, source - expert_count, source)) | (target >= lanes)
    join = jnp.where(
        to_expert & (source < 2 * expert_count), jnp.where(is_low, 1.0, 256.0), 0.0
    ).astype(jnp.bfloat16)
    stats = []

    def run(blocks):
        res = apply_experts(blocks, half, own, join, weights)
        stats.append(res[-1])
        return res[:-1]

    def add(*terms):
        return sum(term.astype(jnp.float32) for term in terms).astype(jnp.bfloat16)

    low, high = right(packed), left(packed)
    outs = {}
    for k in range(1, far + 1):
        if k > 1:
            low, high, outs[k - 1] = tie((low, high, outs[k - 1]))
        here = low, high
        if k == far:
            break
        if k < far - 1:
            low, high = right(low), left(high)
        else:
            low, high = right(low[:half]), left(high[half:])
        outs[k] = run(here)
    res = run(here)

    ways = (left, left, right, right)
    from_far = {0: res[0], 3: res[1]}
    sums = [ways[i](from_far.get(i, outs[far - 1][i])) for i in (1, 2, 0, 3)]
    sums = [sums[(1, 2, 0, 3).index(i)] for i in range(4)]
    for k in range(far - 1, 0, -1):
        if k == max(1, far - 2):
            packed, sums[1] = tie((packed, sums[1]))
            own_rows = run([packed])
        for i in (1, 2, 0, 3):
            step = k if i in from_far else k - 1
            if step:
                sums[i] = ways[i](add(outs[step][i], sums[i]))
    mixed = join_halves((own_rows[0], sums[0], sums[2]), (own_rows[1], sums[1], sums[3]))

    total = sum(stats)
    counts, mass = (total + sibling(total))[:, :expert_count]
    mass = mass / token_total
    own_count = lax.dynamic_slice(counts, (node,), (1,))
    expert_load = own_count * expert_count / (token_total * per_token)
    balance_loss = (expert_count * jnp.sum(counts / (token_total * per_token) * mass)).reshape(1)
    return (mixed, expert_load, balance_loss)


def solution(mesh):
    return jax.shard_map(
        body,
        mesh=mesh,
        in_specs=(
            P(("groups", "node"), None),
            P(("groups", "node"), None),
            P(("groups", "node"), None),
            P("node", None, None),
            P("node", None, None),
            P("node", None, None),
        ),
        out_specs=(P(("groups", "node"), None), P(("groups", "node")), P("groups")),
        check_vma=False,
    )
```

```python
import functools

import jax
import jax.numpy as jnp
from jax import lax
from jax.experimental import pallas as pl
from jax.experimental.pallas import tpu as pltpu
from jax.sharding import PartitionSpec as P

CORES = 2
LANES = 128
VMEM_LIMIT = 10 * 1024 * 1024
HIDDEN_CHUNK = 256
OUT_CHUNK = 512


def ring_order(chips):
    if chips <= 8:
        return list(range(0, chips, 2)) + list(range(1, chips, 2))[::-1]
    return list(range(chips))


def ring_shift(order, step):
    pairs = []
    for place, chip in enumerate(order):
        target = order[(place + step) % len(order)]
        pairs += [(CORES * chip + core, CORES * target + core) for core in range(CORES)]
    return pairs


def turn(array):
    return pltpu.roll(array, LANES // 2, 1)


def pack_kernel(
    tokens_hbm, ids_hbm, gates_hbm, out_ref, tokens_ref, ids_ref, gates_ref, arrived
):
    half = tokens_ref.shape[0] // 2
    columns = tokens_ref.shape[1] // LANES
    experts = out_ref.shape[1] - columns * half
    copies = [
        pltpu.make_async_copy(source, target, arrived.at[i])
        for i, (source, target) in enumerate(
            ((ids_hbm, ids_ref), (gates_hbm, gates_ref), (tokens_hbm, tokens_ref))
        )
    ]
    for copy in copies:
        copy.start()
    copies[0].wait()
    copies[1].wait()
    expert = lax.broadcasted_iota(jnp.int32, (experts, LANES), 0)
    first = lax.broadcasted_iota(jnp.int32, (experts, LANES), 1) < LANES // 2
    scores = jnp.zeros((experts, LANES), jnp.int32)
    for k in range(ids_ref.shape[0]):
        scores = jnp.where(expert == ids_ref[k : k + 1, :], gates_ref[k : k + 1, :], scores)
    high = (scores >> 8).astype(jnp.float32)
    low = (scores & 255).astype(jnp.float32)
    halves = jnp.where(first, high, turn(low)), jnp.where(first, turn(high), low)
    for i in range(2):
        out_ref[i, columns * half :, :] = halves[i].astype(jnp.bfloat16)
    copies[2].wait()
    for i in range(2):
        for j in range(columns):
            out_ref[i, j * half : (j + 1) * half, :] = tokens_ref[
                i * half : (i + 1) * half, j * LANES : (j + 1) * LANES
            ]


def pack(tokens, expert_ids, gate_fixed, experts):
    rows, width = tokens.shape
    per_token = expert_ids.shape[1]
    height = rows // 2 * (width // LANES) + experts
    return pl.pallas_call(
        pack_kernel,
        out_shape=jax.ShapeDtypeStruct((2, height, LANES), jnp.bfloat16),
        in_specs=[pl.BlockSpec(memory_space=pl.ANY)] * 3,
        out_specs=pl.BlockSpec(memory_space=pltpu.VMEM),
        scratch_shapes=[
            pltpu.VMEM((rows, width), jnp.bfloat16),
            pltpu.VMEM((per_token, rows), jnp.int32),
            pltpu.VMEM((per_token, rows), jnp.int32),
            pltpu.SemaphoreType.DMA((3,)),
        ],
        cost_estimate=pl.CostEstimate(
            flops=rows * LANES, bytes_accessed=4 * rows * width, transcendentals=0
        ),
    )(tokens, expert_ids.T, gate_fixed.T)


def join_kernel(*refs):
    out_ref = refs[-1]
    half = out_ref.shape[0] // 2
    for i in range(2):
        total = sum(ref[...].astype(jnp.float32) for ref in refs[3 * i : 3 * i + 3])
        out_ref[i * half : (i + 1) * half, :] = total.astype(jnp.bfloat16)


def join_halves(first, second):
    rows, width = first[0].shape
    in_vmem = pl.BlockSpec(memory_space=pltpu.VMEM)
    return pl.pallas_call(
        join_kernel,
        out_shape=jax.ShapeDtypeStruct((2 * rows, width), jnp.bfloat16),
        in_specs=[in_vmem] * 6,
        out_specs=in_vmem,
        compiler_params=pltpu.CompilerParams(vmem_limit_bytes=VMEM_LIMIT // 2),
    )(*first, *second)


def hold_kernel(*refs):
    count = len(refs) // 2
    arrived = refs[-1]
    copies = [
        pltpu.make_async_copy(refs[i], refs[count + i], arrived.at[i]) for i in range(count)
    ]
    for copy in copies:
        copy.start()
    for copy in copies:
        copy.wait()


def hold(arrays):
    return pl.pallas_call(
        hold_kernel,
        out_shape=[pltpu.VMEM(array.shape, array.dtype) for array in arrays],
        in_specs=[pl.BlockSpec(memory_space=pl.ANY)] * len(arrays),
        out_specs=[pl.BlockSpec(memory_space=pltpu.VMEM)] * len(arrays),
        scratch_shapes=[pltpu.SemaphoreType.DMA((len(arrays),))],
        compiler_params=pltpu.CompilerParams(vmem_limit_bytes=VMEM_LIMIT),
    )(*arrays)


def expert_kernel(count, piece, *refs):
    halves = []
    for ref in refs[:count]:
        halves += [ref] if len(ref.shape) == 2 else [ref.at[0], ref.at[1]]
    own_ref = refs[count]
    experts = [refs[count + 1 + 3 * i : count + 4 + 3 * i] for i in range(CORES)]
    *outs, stats_ref, hidden_ref = refs[count + 1 + 3 * CORES :]
    width, hidden_width = experts[0][0].shape
    columns = width // LANES

    scores = [half[columns * piece :, :].astype(jnp.float32) for half in halves]
    scores = [256.0 * score + turn(score) for score in scores]
    first = lax.broadcasted_iota(jnp.int32, scores[0].shape, 1) < LANES // 2
    scores = jnp.concatenate(
        [
            jnp.where(first, scores[i], turn(scores[i + 1]))
            for i in range(0, len(scores), 2)
        ],
        axis=1,
    )
    dense = scores / jnp.sum(scores, axis=0, keepdims=True)
    idle = jnp.zeros((LANES - dense.shape[0], dense.shape[1]), jnp.float32)
    weights = jnp.concatenate([dense, idle], axis=0).T
    stats_ref[0:1, :] = jnp.sum((weights > 0).astype(jnp.float32), axis=0, keepdims=True)
    stats_ref[1:2, :] = jnp.sum(weights, axis=0, keepdims=True)
    scales = [
        jnp.sum(weights * own_ref[i : i + 1, :], axis=1, keepdims=True) for i in range(CORES)
    ]

    rows = jnp.concatenate(
        [
            jnp.concatenate([half[j * piece : (j + 1) * piece, :] for half in halves], axis=0)
            for j in range(columns)
        ],
        axis=1,
    )
    for i, (gate_ref, up_ref, _) in enumerate(experts):
        for start in range(0, hidden_width, HIDDEN_CHUNK):
            at = slice(start, start + HIDDEN_CHUNK)
            gate = jnp.dot(rows, gate_ref[:, at], preferred_element_type=jnp.float32)
            up = jnp.dot(rows, up_ref[:, at], preferred_element_type=jnp.float32)
            hidden_ref[i, :, at] = (gate / (1.0 + jnp.exp(-gate)) * up).astype(jnp.bfloat16)
    for start in range(0, width, OUT_CHUNK):
        at = slice(start, start + OUT_CHUNK)
        total = 0.0
        for i, (_, _, down_ref) in enumerate(experts):
            out = jnp.dot(hidden_ref[i], down_ref[:, at], preferred_element_type=jnp.float32)
            total = total + out.astype(jnp.bfloat16).astype(jnp.float32) * scales[i]
        for i, out_ref in enumerate(outs):
            out_ref[:, at] = total[i * piece : (i + 1) * piece].astype(jnp.bfloat16)


def apply_experts(blocks, piece, own, weights):
    width, hidden_width = weights[0].shape
    count = len(blocks)
    total = piece * sum(1 if block.ndim == 2 else 2 for block in blocks)
    in_vmem = pl.BlockSpec(memory_space=pltpu.VMEM)
    return pl.pallas_call(
        functools.partial(expert_kernel, count, piece),
        out_shape=[jax.ShapeDtypeStruct((piece, width), jnp.bfloat16)] * (total // piece)
        + [jax.ShapeDtypeStruct((2, own.shape[1]), jnp.float32)],
        in_specs=[in_vmem] * (count + 1 + len(weights)),
        out_specs=[in_vmem] * (total // piece + 1),
        scratch_shapes=[pltpu.VMEM((CORES, total, hidden_width), jnp.bfloat16)],
        compiler_params=pltpu.CompilerParams(vmem_limit_bytes=VMEM_LIMIT),
        cost_estimate=pl.CostEstimate(
            flops=6 * CORES * total * width * hidden_width,
            bytes_accessed=4 * total * width,
            transcendentals=CORES * total * hidden_width,
        ),
    )(*blocks, own, *weights)


def body(tokens, expert_ids, gate_fixed, gate_weight, up_weight, down_weight):
    tok_rows, model_width = tokens.shape
    per_token = expert_ids.shape[1]
    node_count = lax.axis_size("node")
    expert_count = node_count
    token_total = tok_rows * node_count
    chips = node_count // CORES
    far = chips // 2
    half = tok_rows // 2
    order = ring_order(chips)
    to_right, to_left = ring_shift(order, 1), ring_shift(order, -1)
    to_sibling = [(node, node ^ 1) for node in range(node_count)]
    right = lambda a: lax.ppermute(a, "node", to_right)
    left = lambda a: lax.ppermute(a, "node", to_left)
    sibling = lambda a: lax.ppermute(a, "node", to_sibling)
    tie = lax.optimization_barrier
    node = lax.axis_index("node")

    weights = [gate_weight[0], up_weight[0], down_weight[0]]
    others = [sibling(weight) for weight in weights]
    weights = hold([pltpu.with_memory_space_constraint(w, pltpu.HBM) for w in weights + others])
    packed = pack(tokens, expert_ids, gate_fixed, expert_count)
    own = (jnp.arange(LANES)[None] == jnp.stack([node, node ^ 1])[:, None]).astype(jnp.float32)
    stats = []

    def run(blocks):
        res = apply_experts(blocks, half, own, weights)
        stats.append(res[-1])
        return res[:-1]

    def add(*terms):
        return sum(term.astype(jnp.float32) for term in terms).astype(jnp.bfloat16)

    low, high = right(packed), left(packed)
    outs = {}
    for k in range(1, far + 1):
        if k > 1:
            low, high, outs[k - 1] = tie((low, high, outs[k - 1]))
        here = low, high
        if k == far:
            break
        if k < far - 1:
            low, high = right(low), left(high)
        else:
            low, high = right(low[0]), left(high[1])
        outs[k] = run(here)
    res = run(here)

    ways = (left, left, right, right)
    from_far = {0: res[0], 3: res[1]}
    sums = [ways[i](from_far.get(i, outs[far - 1][i])) for i in (1, 2, 0, 3)]
    sums = [sums[(1, 2, 0, 3).index(i)] for i in range(4)]
    for k in range(far - 1, 0, -1):
        if k == max(1, far - 2):
            packed, sums[1] = tie((packed, sums[1]))
            own_rows = run([packed])
        for i in (1, 2, 0, 3):
            step = k if i in from_far else k - 1
            if step:
                sums[i] = ways[i](add(outs[step][i], sums[i]))
    mixed = join_halves((own_rows[0], sums[0], sums[2]), (own_rows[1], sums[1], sums[3]))

    total = sum(stats)
    counts, mass = (total + sibling(total))[:, :expert_count]
    mass = mass / token_total
    own_count = lax.dynamic_slice(counts, (node,), (1,))
    expert_load = own_count * expert_count / (token_total * per_token)
    balance_loss = (expert_count * jnp.sum(counts / (token_total * per_token) * mass)).reshape(1)
    return (mixed, expert_load, balance_loss)


def solution(mesh):
    return jax.shard_map(
        body,
        mesh=mesh,
        in_specs=(
            P(("groups", "node"), None),
            P(("groups", "node"), None),
            P(("groups", "node"), None),
            P("node", None, None),
            P("node", None, None),
            P("node", None, None),
        ),
        out_specs=(P(("groups", "node"), None), P(("groups", "node")), P("groups")),
        check_vma=False,
    )
```

```python
import functools

import jax
import jax.numpy as jnp
from jax import lax
from jax.experimental import pallas as pl
from jax.experimental.pallas import tpu as pltpu
from jax.sharding import PartitionSpec as P

CORES = 2
LANES = 128
VMEM_LIMIT = 10 * 1024 * 1024
HIDDEN_CHUNK = 256
OUT_CHUNK = 512


def ring_order(chips):
    if chips <= 8:
        return list(range(0, chips, 2)) + list(range(1, chips, 2))[::-1]
    return list(range(chips))


def ring_shift(order, step):
    pairs = []
    for place, chip in enumerate(order):
        target = order[(place + step) % len(order)]
        pairs += [(CORES * chip + core, CORES * target + core) for core in range(CORES)]
    return pairs


def turn(array):
    return pltpu.roll(array, LANES // 2, 1)


def pack_kernel(
    tokens_hbm, ids_hbm, gates_hbm, out_ref, tokens_ref, ids_ref, gates_ref, arrived
):
    half = tokens_ref.shape[0] // 2
    columns = tokens_ref.shape[1] // LANES
    experts = out_ref.shape[1] - columns * half
    copies = [
        pltpu.make_async_copy(source, target, arrived.at[i])
        for i, (source, target) in enumerate(
            ((ids_hbm, ids_ref), (gates_hbm, gates_ref), (tokens_hbm, tokens_ref))
        )
    ]
    for copy in copies:
        copy.start()
    copies[0].wait()
    copies[1].wait()
    expert = lax.broadcasted_iota(jnp.int32, (experts, LANES), 0)
    first = lax.broadcasted_iota(jnp.int32, (experts, LANES), 1) < LANES // 2
    scores = jnp.zeros((experts, LANES), jnp.int32)
    for k in range(ids_ref.shape[0]):
        scores = jnp.where(expert == ids_ref[k : k + 1, :], gates_ref[k : k + 1, :], scores)
    high = (scores >> 8).astype(jnp.float32)
    low = (scores & 255).astype(jnp.float32)
    halves = jnp.where(first, high, turn(low)), jnp.where(first, turn(high), low)
    for i in range(2):
        out_ref[i, columns * half :, :] = halves[i].astype(jnp.bfloat16)
    copies[2].wait()
    for i in range(2):
        for j in range(columns):
            out_ref[i, j * half : (j + 1) * half, :] = tokens_ref[
                i * half : (i + 1) * half, j * LANES : (j + 1) * LANES
            ]


def pack(tokens, expert_ids, gate_fixed, experts):
    rows, width = tokens.shape
    per_token = expert_ids.shape[1]
    height = rows // 2 * (width // LANES) + experts
    return pl.pallas_call(
        pack_kernel,
        out_shape=jax.ShapeDtypeStruct((2, height, LANES), jnp.bfloat16),
        in_specs=[pl.BlockSpec(memory_space=pl.ANY)] * 3,
        out_specs=pl.BlockSpec(memory_space=pltpu.VMEM),
        scratch_shapes=[
            pltpu.VMEM((rows, width), jnp.bfloat16),
            pltpu.VMEM((per_token, rows), jnp.int32),
            pltpu.VMEM((per_token, rows), jnp.int32),
            pltpu.SemaphoreType.DMA((3,)),
        ],
        cost_estimate=pl.CostEstimate(
            flops=rows * LANES, bytes_accessed=4 * rows * width, transcendentals=0
        ),
    )(tokens, expert_ids.T, gate_fixed.T)


def join_kernel(*refs):
    out_ref = refs[-1]
    half = out_ref.shape[0] // 2
    for i in range(2):
        total = sum(ref[...].astype(jnp.float32) for ref in refs[3 * i : 3 * i + 3])
        out_ref[i * half : (i + 1) * half, :] = total.astype(jnp.bfloat16)


def join_halves(first, second):
    rows, width = first[0].shape
    in_vmem = pl.BlockSpec(memory_space=pltpu.VMEM)
    return pl.pallas_call(
        join_kernel,
        out_shape=jax.ShapeDtypeStruct((2 * rows, width), jnp.bfloat16),
        in_specs=[in_vmem] * 6,
        out_specs=in_vmem,
        compiler_params=pltpu.CompilerParams(vmem_limit_bytes=VMEM_LIMIT // 2),
    )(*first, *second)


def hold_kernel(*refs):
    count = len(refs) // 2
    arrived = refs[-1]
    copies = [
        pltpu.make_async_copy(refs[i], refs[count + i], arrived.at[i]) for i in range(count)
    ]
    for copy in copies:
        copy.start()
    for copy in copies:
        copy.wait()


def hold(arrays):
    return pl.pallas_call(
        hold_kernel,
        out_shape=[pltpu.VMEM(array.shape, array.dtype) for array in arrays],
        in_specs=[pl.BlockSpec(memory_space=pl.ANY)] * len(arrays),
        out_specs=[pl.BlockSpec(memory_space=pltpu.VMEM)] * len(arrays),
        scratch_shapes=[pltpu.SemaphoreType.DMA((len(arrays),))],
        compiler_params=pltpu.CompilerParams(vmem_limit_bytes=VMEM_LIMIT),
    )(*arrays)


def expert_kernel(count, piece, *refs):
    halves = []
    for ref in refs[:count]:
        halves += [ref] if len(ref.shape) == 2 else [ref.at[0], ref.at[1]]
    own_ref = refs[count]
    experts = [refs[count + 1 + 3 * i : count + 4 + 3 * i] for i in range(CORES)]
    *outs, stats_ref, hidden_ref = refs[count + 1 + 3 * CORES :]
    width, hidden_width = experts[0][0].shape
    columns = width // LANES

    scores = [half[columns * piece :, :].astype(jnp.float32) for half in halves]
    scores = [256.0 * score + turn(score) for score in scores]
    first = lax.broadcasted_iota(jnp.int32, scores[0].shape, 1) < LANES // 2
    scores = jnp.concatenate(
        [
            jnp.where(first, scores[i], turn(scores[i + 1]))
            for i in range(0, len(scores), 2)
        ],
        axis=1,
    )
    dense = scores / jnp.sum(scores, axis=0, keepdims=True)
    idle = jnp.zeros((LANES - dense.shape[0], dense.shape[1]), jnp.float32)
    weights = jnp.concatenate([dense, idle], axis=0).T
    stats_ref[0:1, :] = jnp.sum((weights > 0).astype(jnp.float32), axis=0, keepdims=True)
    stats_ref[1:2, :] = jnp.sum(weights, axis=0, keepdims=True)
    scales = [
        jnp.sum(weights * own_ref[i : i + 1, :], axis=1, keepdims=True) for i in range(CORES)
    ]

    rows = jnp.concatenate(
        [
            jnp.concatenate([half[j * piece : (j + 1) * piece, :] for half in halves], axis=0)
            for j in range(columns)
        ],
        axis=1,
    )
    for i, (gate_ref, up_ref, _) in enumerate(experts):
        for start in range(0, hidden_width, HIDDEN_CHUNK):
            at = slice(start, start + HIDDEN_CHUNK)
            gate = jnp.dot(rows, gate_ref[:, at], preferred_element_type=jnp.float32)
            up = jnp.dot(rows, up_ref[:, at], preferred_element_type=jnp.float32)
            hidden_ref[i, :, at] = (gate / (1.0 + jnp.exp(-gate)) * up).astype(jnp.bfloat16)
    for start in range(0, width, OUT_CHUNK):
        at = slice(start, start + OUT_CHUNK)
        total = 0.0
        for i, (_, _, down_ref) in enumerate(experts):
            out = jnp.dot(hidden_ref[i], down_ref[:, at], preferred_element_type=jnp.float32)
            total = total + out.astype(jnp.bfloat16).astype(jnp.float32) * scales[i]
        for i, out_ref in enumerate(outs):
            out_ref[:, at] = total[i * piece : (i + 1) * piece].astype(jnp.bfloat16)


def apply_experts(blocks, piece, own, weights):
    width, hidden_width = weights[0].shape
    count = len(blocks)
    total = piece * sum(1 if block.ndim == 2 else 2 for block in blocks)
    in_vmem = pl.BlockSpec(memory_space=pltpu.VMEM)
    return pl.pallas_call(
        functools.partial(expert_kernel, count, piece),
        out_shape=[jax.ShapeDtypeStruct((piece, width), jnp.bfloat16)] * (total // piece)
        + [jax.ShapeDtypeStruct((2, own.shape[1]), jnp.float32)],
        in_specs=[in_vmem] * (count + 1 + len(weights)),
        out_specs=[in_vmem] * (total // piece + 1),
        scratch_shapes=[pltpu.VMEM((CORES, total, hidden_width), jnp.bfloat16)],
        compiler_params=pltpu.CompilerParams(vmem_limit_bytes=VMEM_LIMIT),
        cost_estimate=pl.CostEstimate(
            flops=6 * CORES * total * width * hidden_width,
            bytes_accessed=4 * total * width,
            transcendentals=CORES * total * hidden_width,
        ),
    )(*blocks, own, *weights)


def body(tokens, expert_ids, gate_fixed, gate_weight, up_weight, down_weight):
    tok_rows, model_width = tokens.shape
    per_token = expert_ids.shape[1]
    node_count = lax.axis_size("node")
    expert_count = node_count
    token_total = tok_rows * node_count
    chips = node_count // CORES
    far = chips // 2
    half = tok_rows // 2
    order = ring_order(chips)
    to_right, to_left = ring_shift(order, 1), ring_shift(order, -1)
    to_sibling = [(node, node ^ 1) for node in range(node_count)]
    right = lambda a: lax.ppermute(a, "node", to_right)
    left = lambda a: lax.ppermute(a, "node", to_left)
    sibling = lambda a: lax.ppermute(a, "node", to_sibling)
    tie = lax.optimization_barrier
    node = lax.axis_index("node")

    weights = [gate_weight[0], up_weight[0], down_weight[0]]
    others = [sibling(weight) for weight in weights]
    weights = hold([pltpu.with_memory_space_constraint(w, pltpu.HBM) for w in weights + others])
    packed = pack(tokens, expert_ids, gate_fixed, expert_count)
    own = (jnp.arange(LANES)[None] == jnp.stack([node, node ^ 1])[:, None]).astype(jnp.float32)
    stats = []

    def run(blocks):
        res = apply_experts(blocks, half, own, weights)
        stats.append(res[-1])
        return res[:-1]

    def add(*terms):
        return sum(term.astype(jnp.float32) for term in terms).astype(jnp.bfloat16)

    low, high = right(packed), left(packed)
    outs = {}
    for k in range(1, far + 1):
        if k > 1:
            low, high, outs[k - 1] = tie((low, high, outs[k - 1]))
        here = low, high
        if k == far:
            break
        if k < far - 1:
            low, high = right(low), left(high)
        else:
            low, high = right(low[0]), left(high[1])
        outs[k] = run(here)
    res = run(here)

    ways = (left, left, right, right)
    from_far = {0: res[0], 3: res[1]}
    sums = [ways[i](from_far.get(i, outs[far - 1][i])) for i in (2, 1, 3, 0)]
    sums = [sums[(2, 1, 3, 0).index(i)] for i in range(4)]
    for k in range(far - 1, 0, -1):
        if k == max(1, far - 2):
            packed, sums[1] = tie((packed, sums[1]))
            own_rows = run([packed])
        for i in (2, 1, 3, 0):
            step = k if i in from_far else k - 1
            if step:
                sums[i] = ways[i](add(outs[step][i], sums[i]))
    mixed = join_halves((own_rows[0], sums[0], sums[2]), (own_rows[1], sums[1], sums[3]))

    total = sum(stats)
    counts, mass = (total + sibling(total))[:, :expert_count]
    mass = mass / token_total
    own_count = lax.dynamic_slice(counts, (node,), (1,))
    expert_load = own_count * expert_count / (token_total * per_token)
    balance_loss = (expert_count * jnp.sum(counts / (token_total * per_token) * mass)).reshape(1)
    return (mixed, expert_load, balance_loss)


def solution(mesh):
    return jax.shard_map(
        body,
        mesh=mesh,
        in_specs=(
            P(("groups", "node"), None),
            P(("groups", "node"), None),
            P(("groups", "node"), None),
            P("node", None, None),
            P("node", None, None),
            P("node", None, None),
        ),
        out_specs=(P(("groups", "node"), None), P(("groups", "node")), P("groups")),
        check_vma=False,
    )
```

```python
import functools

import jax
import jax.numpy as jnp
from jax import lax
from jax.experimental import pallas as pl
from jax.experimental.pallas import tpu as pltpu
from jax.sharding import PartitionSpec as P

CORES = 2
LANES = 128
VMEM_LIMIT = 10 * 1024 * 1024
HIDDEN_CHUNK = 256
OUT_CHUNK = 512


def ring_order(chips):
    if chips <= 8:
        return list(range(0, chips, 2)) + list(range(1, chips, 2))[::-1]
    return list(range(chips))


def ring_shift(order, step):
    pairs = []
    for place, chip in enumerate(order):
        target = order[(place + step) % len(order)]
        pairs += [(CORES * chip + core, CORES * target + core) for core in range(CORES)]
    return pairs


def turn(array):
    return pltpu.roll(array, LANES // 2, 1)


def pack_kernel(
    tokens_hbm, ids_hbm, gates_hbm, out_ref, tokens_ref, ids_ref, gates_ref, arrived
):
    half = tokens_ref.shape[0] // 2
    columns = tokens_ref.shape[1] // LANES
    experts = out_ref.shape[1] - columns * half
    copies = [
        pltpu.make_async_copy(source, target, arrived.at[i])
        for i, (source, target) in enumerate(
            ((ids_hbm, ids_ref), (gates_hbm, gates_ref), (tokens_hbm, tokens_ref))
        )
    ]
    for copy in copies:
        copy.start()
    copies[0].wait()
    copies[1].wait()
    expert = lax.broadcasted_iota(jnp.int32, (experts, LANES), 0)
    first = lax.broadcasted_iota(jnp.int32, (experts, LANES), 1) < LANES // 2
    scores = jnp.zeros((experts, LANES), jnp.int32)
    for k in range(ids_ref.shape[0]):
        scores = jnp.where(expert == ids_ref[k : k + 1, :], gates_ref[k : k + 1, :], scores)
    high = (scores >> 8).astype(jnp.float32)
    low = (scores & 255).astype(jnp.float32)
    halves = jnp.where(first, high, turn(low)), jnp.where(first, turn(high), low)
    for i in range(2):
        out_ref[i, columns * half :, :] = halves[i].astype(jnp.bfloat16)
    copies[2].wait()
    for i in range(2):
        for j in range(columns):
            out_ref[i, j * half : (j + 1) * half, :] = tokens_ref[
                i * half : (i + 1) * half, j * LANES : (j + 1) * LANES
            ]


def pack(tokens, expert_ids, gate_fixed, experts):
    rows, width = tokens.shape
    per_token = expert_ids.shape[1]
    height = rows // 2 * (width // LANES) + experts
    return pl.pallas_call(
        pack_kernel,
        out_shape=jax.ShapeDtypeStruct((2, height, LANES), jnp.bfloat16),
        in_specs=[pl.BlockSpec(memory_space=pl.ANY)] * 3,
        out_specs=pl.BlockSpec(memory_space=pltpu.VMEM),
        scratch_shapes=[
            pltpu.VMEM((rows, width), jnp.bfloat16),
            pltpu.VMEM((per_token, rows), jnp.int32),
            pltpu.VMEM((per_token, rows), jnp.int32),
            pltpu.SemaphoreType.DMA((3,)),
        ],
        cost_estimate=pl.CostEstimate(
            flops=rows * LANES, bytes_accessed=4 * rows * width, transcendentals=0
        ),
    )(tokens, expert_ids.T, gate_fixed.T)


def join_kernel(*refs):
    out_ref = refs[-1]
    half = out_ref.shape[0] // 2
    for i in range(2):
        total = sum(ref[...].astype(jnp.float32) for ref in refs[3 * i : 3 * i + 3])
        out_ref[i * half : (i + 1) * half, :] = total.astype(jnp.bfloat16)


def join_halves(first, second):
    rows, width = first[0].shape
    in_vmem = pl.BlockSpec(memory_space=pltpu.VMEM)
    return pl.pallas_call(
        join_kernel,
        out_shape=jax.ShapeDtypeStruct((2 * rows, width), jnp.bfloat16),
        in_specs=[in_vmem] * 6,
        out_specs=in_vmem,
        compiler_params=pltpu.CompilerParams(vmem_limit_bytes=VMEM_LIMIT // 2),
    )(*first, *second)


def hold_kernel(*refs):
    count = len(refs) // 2 - 1
    mark_ref, arrived = refs[-2:]
    mark_ref[...] = jnp.zeros(mark_ref.shape, mark_ref.dtype)
    copies = [
        pltpu.make_async_copy(refs[i], refs[count + i], arrived.at[i]) for i in range(count)
    ]
    for copy in copies:
        copy.start()
    for copy in copies:
        copy.wait()


def hold(arrays):
    return pl.pallas_call(
        hold_kernel,
        out_shape=[pltpu.VMEM(array.shape, array.dtype) for array in arrays]
        + [jax.ShapeDtypeStruct((2, LANES), jnp.float32)],
        in_specs=[pl.BlockSpec(memory_space=pl.ANY)] * len(arrays),
        out_specs=[pl.BlockSpec(memory_space=pltpu.VMEM)] * (len(arrays) + 1),
        scratch_shapes=[pltpu.SemaphoreType.DMA((len(arrays),))],
        compiler_params=pltpu.CompilerParams(vmem_limit_bytes=VMEM_LIMIT),
    )(*arrays)


def expert_kernel(count, piece, *refs):
    halves = []
    for ref in refs[:count]:
        halves += [ref] if len(ref.shape) == 2 else [ref.at[0], ref.at[1]]
    own_ref = refs[count]
    experts = [refs[count + 1 + 3 * i : count + 4 + 3 * i] for i in range(CORES)]
    *outs, stats_ref, hidden_ref = refs[count + 1 + 3 * CORES :]
    width, hidden_width = experts[0][0].shape
    columns = width // LANES

    scores = [half[columns * piece :, :].astype(jnp.float32) for half in halves]
    scores = [256.0 * score + turn(score) for score in scores]
    first = lax.broadcasted_iota(jnp.int32, scores[0].shape, 1) < LANES // 2
    scores = jnp.concatenate(
        [
            jnp.where(first, scores[i], turn(scores[i + 1]))
            for i in range(0, len(scores), 2)
        ],
        axis=1,
    )
    dense = scores / jnp.sum(scores, axis=0, keepdims=True)
    idle = jnp.zeros((LANES - dense.shape[0], dense.shape[1]), jnp.float32)
    weights = jnp.concatenate([dense, idle], axis=0).T
    stats_ref[0:1, :] = jnp.sum((weights > 0).astype(jnp.float32), axis=0, keepdims=True)
    stats_ref[1:2, :] = jnp.sum(weights, axis=0, keepdims=True)
    scales = [
        jnp.sum(weights * own_ref[i : i + 1, :], axis=1, keepdims=True) for i in range(CORES)
    ]

    rows = jnp.concatenate(
        [
            jnp.concatenate([half[j * piece : (j + 1) * piece, :] for half in halves], axis=0)
            for j in range(columns)
        ],
        axis=1,
    )
    for i, (gate_ref, up_ref, _) in enumerate(experts):
        for start in range(0, hidden_width, HIDDEN_CHUNK):
            at = slice(start, start + HIDDEN_CHUNK)
            gate = jnp.dot(rows, gate_ref[:, at], preferred_element_type=jnp.float32)
            up = jnp.dot(rows, up_ref[:, at], preferred_element_type=jnp.float32)
            hidden_ref[i, :, at] = (gate / (1.0 + jnp.exp(-gate)) * up).astype(jnp.bfloat16)
    for start in range(0, width, OUT_CHUNK):
        at = slice(start, start + OUT_CHUNK)
        total = 0.0
        for i, (_, _, down_ref) in enumerate(experts):
            out = jnp.dot(hidden_ref[i], down_ref[:, at], preferred_element_type=jnp.float32)
            total = total + out.astype(jnp.bfloat16).astype(jnp.float32) * scales[i]
        for i, out_ref in enumerate(outs):
            out_ref[:, at] = total[i * piece : (i + 1) * piece].astype(jnp.bfloat16)


def apply_experts(blocks, piece, own, weights):
    width, hidden_width = weights[0].shape
    count = len(blocks)
    total = piece * sum(1 if block.ndim == 2 else 2 for block in blocks)
    in_vmem = pl.BlockSpec(memory_space=pltpu.VMEM)
    return pl.pallas_call(
        functools.partial(expert_kernel, count, piece),
        out_shape=[jax.ShapeDtypeStruct((piece, width), jnp.bfloat16)] * (total // piece)
        + [jax.ShapeDtypeStruct((2, own.shape[1]), jnp.float32)],
        in_specs=[in_vmem] * (count + 1 + len(weights)),
        out_specs=[in_vmem] * (total // piece + 1),
        scratch_shapes=[pltpu.VMEM((CORES, total, hidden_width), jnp.bfloat16)],
        compiler_params=pltpu.CompilerParams(vmem_limit_bytes=VMEM_LIMIT),
        cost_estimate=pl.CostEstimate(
            flops=6 * CORES * total * width * hidden_width,
            bytes_accessed=4 * total * width,
            transcendentals=CORES * total * hidden_width,
        ),
    )(*blocks, own, *weights)


def body(tokens, expert_ids, gate_fixed, gate_weight, up_weight, down_weight):
    tok_rows, model_width = tokens.shape
    per_token = expert_ids.shape[1]
    node_count = lax.axis_size("node")
    expert_count = node_count
    token_total = tok_rows * node_count
    chips = node_count // CORES
    far = chips // 2
    half = tok_rows // 2
    order = ring_order(chips)
    to_right, to_left = ring_shift(order, 1), ring_shift(order, -1)
    to_sibling = [(node, node ^ 1) for node in range(node_count)]
    right = lambda a: lax.ppermute(a, "node", to_right)
    left = lambda a: lax.ppermute(a, "node", to_left)
    sibling = lambda a: lax.ppermute(a, "node", to_sibling)
    tie = lax.optimization_barrier
    node = lax.axis_index("node")

    weights = [gate_weight[0], up_weight[0], down_weight[0]]
    others = [sibling(weight) for weight in weights]
    *weights, held = hold([pltpu.with_memory_space_constraint(w, pltpu.HBM) for w in weights + others])
    packed = pack(tokens, expert_ids, gate_fixed, expert_count)
    own = (jnp.arange(LANES)[None] == jnp.stack([node, node ^ 1])[:, None]).astype(jnp.float32)
    stats = [held]

    def run(blocks):
        res = apply_experts(blocks, half, own, weights)
        stats.append(res[-1])
        return res[:-1]

    def add(*terms):
        return sum(term.astype(jnp.float32) for term in terms).astype(jnp.bfloat16)

    low, high = right(packed), left(packed)
    blocks, outs, fresh = {}, {}, {}
    for k in range(1, far + 1):
        if k == 2:
            low, high, stats[0] = tie((low, high, stats[0]))
        elif k > 2:
            low, high, fresh = tie((low, high, fresh))
            outs.update(fresh)
        here = blocks[k] = [low, high]
        if k == far:
            break
        if k < far - 1:
            low, high = right(low), left(high)
        else:
            low, high = right(low[0]), left(high[1])
        ready = [i for i in blocks if i not in outs] if k >= min(2, far - 1) else []
        fresh = {i: run(blocks[i]) for i in ready}
    res = run(here)

    ways = (left, left, right, right)
    from_far = {0: res[0], 3: res[1]}
    sums = [ways[i](from_far.get(i, outs[far - 1][i])) for i in (1, 2, 0, 3)]
    sums = [sums[(1, 2, 0, 3).index(i)] for i in range(4)]
    for k in range(far - 1, 0, -1):
        if k == max(1, far - 2):
            packed, sums[1] = tie((packed, sums[1]))
            own_rows = run([packed])
        for i in (1, 2, 0, 3):
            step = k if i in from_far else k - 1
            if step:
                sums[i] = ways[i](add(outs[step][i], sums[i]))
    mixed = join_halves((own_rows[0], sums[0], sums[2]), (own_rows[1], sums[1], sums[3]))

    total = sum(stats)
    counts, mass = (total + sibling(total))[:, :expert_count]
    mass = mass / token_total
    own_count = lax.dynamic_slice(counts, (node,), (1,))
    expert_load = own_count * expert_count / (token_total * per_token)
    balance_loss = (expert_count * jnp.sum(counts / (token_total * per_token) * mass)).reshape(1)
    return (mixed, expert_load, balance_loss)


def solution(mesh):
    return jax.shard_map(
        body,
        mesh=mesh,
        in_specs=(
            P(("groups", "node"), None),
            P(("groups", "node"), None),
            P(("groups", "node"), None),
            P("node", None, None),
            P("node", None, None),
            P("node", None, None),
        ),
        out_specs=(P(("groups", "node"), None), P(("groups", "node")), P("groups")),
        check_vma=False,
    )
```
